32 devices in a mesh: blk: 8 (over z, y), tower: 4 (over x, core).
Axes of the slice: x: 2, y: 2, z: 4, core: 2. Of those that a mesh axis runs over, the one named last changes fastest.
Arguments:
- layer_input: bfloat16 [16384, 1152], P(('blk', 'tower')), may hold values from -8 to 8
- caption_ids: int32 [64, 64], P('blk'), may hold values from 0 to 31999, as said below
- positives: int32 [48], P('blk'), may hold values from 0 to 63, as said below
- ln_gain: float32 [2, 1152], replicated, may hold values from 0.1 to 1.9
- w_first: bfloat16 [2, 1152, 2176], P(None, None, 'blk'), may hold values from -0.1875 to 0.1875
- w_second: bfloat16 [2, 2176, 1152], P(None, 'blk'), may hold values from -0.125 to 0.125
- logit_scale: float32 [1], replicated, may hold values from 20 to 80
- logit_bias: float32 [1], replicated, may hold values from -6 to -2
Outputs:
- input_grad: float32 [16384, 1152], P(('blk', 'tower'))
The draws below stay inside these ranges and needn't reach their ends.
Inputs may be any that keep to these rules, and one draw needn't show every extreme that they name: `caption_ids`: each caption's ids are nonzero for its first 32 or more positions and zero after; some caption has no zeros. `positives`: no two images have the same positive caption.
All inputs are finite; a program needn't handle non-finite values.
Results may differ from the reference program's by a relative error of at most 0.013.
Values may be sent and summed in bfloat16 or wider, within the bound.
No kernel may reach another device: no remote copies, remote signals or barrier semaphores. Data moves between devices by JAX's collectives and lax.ppermute only.
A program may use at most 128 MiB of HBM per device.

```python
import math
import jax
import jax.numpy as jnp
from jax import lax

D = 1152
PATCHES = 256
TEXT_LEN = 64
VOCAB = 32000
FFW = 2176
IMG_DEV = 2
ROWS = 512
CAP_DEV = 8
IMAGES = 48
CAPTIONS = 64
N_BLK = 8
N_TOWER = 4


def pairing(key):
    return jax.random.permutation(key, CAPTIONS)


def draw_positives(key, part):
    chosen = pairing(key)
    return chosen[:IMAGES].astype(jnp.int32)


def draw_caption_ids(key, part):
    key = jax.random.fold_in(key, 23)
    key_len, key_tok = jax.random.split(key)
    lengths = jax.random.randint(key_len, (CAPTIONS,), TEXT_LEN // 2, TEXT_LEN + 1)
    lengths = lengths.at[0].set(TEXT_LEN)
    tokens = jax.random.randint(key_tok, (CAPTIONS, TEXT_LEN), 1, VOCAB)
    position = jnp.arange(TEXT_LEN)[None, :]
    return jnp.where(position < lengths[:, None], tokens, 0).astype(jnp.int32)


def draw_layer_input(key, part):
    chosen = pairing(key)[:IMAGES]
    key = jax.random.fold_in(key, 31)
    key_cap, key_img, key_noise = jax.random.split(key, 3)
    caption_dir = jax.random.normal(key_cap, (CAPTIONS, D), jnp.float32)
    own_dir = jax.random.normal(key_img, (IMAGES, D), jnp.float32)
    share = 0.25
    noise = jax.random.normal(key_noise, (N_BLK, N_TOWER, ROWS, D), jnp.float32)
    image_offset = share * caption_dir[chosen] + math.sqrt(1.0 - share * share) * own_dir
    image_part = jnp.broadcast_to(image_offset.reshape(N_BLK, N_TOWER - 1, IMG_DEV, 1, D), (N_BLK, N_TOWER - 1, IMG_DEV, PATCHES, D))
    image_part = image_part.reshape(N_BLK, N_TOWER - 1, ROWS, D)
    text_part = jnp.broadcast_to(caption_dir.reshape(N_BLK, 1, CAP_DEV, 1, D), (N_BLK, 1, CAP_DEV, TEXT_LEN, D))
    text_part = text_part.reshape(N_BLK, 1, ROWS, D)
    offsets = jnp.concatenate([image_part, text_part], axis=1)
    values = jnp.clip(offsets + noise, -8.0, 8.0)
    return values.reshape(N_BLK * N_TOWER * ROWS, D).astype(jnp.bfloat16)


def levels(rng, shape, shards, least, largest):
    def one(dim, shards_of):
        heights = jax.random.uniform(jax.random.fold_in(jax.random.fold_in(rng, 6), dim), (shards_of,), jnp.float32, least / len(shards), largest / len(shards))
        return jnp.repeat(jnp.exp(heights), shape[dim] // shards_of).reshape((-1,) + (1,) * (len(shape) - dim - 1))

    level = one(*shards[0])
    for cut in shards[1:]:
        level = level * one(*cut)
    return level


def normal_values(rng, extent, width, most, shards=(), held_as=jnp.bfloat16):
    level = levels(rng, extent, shards, -0.22, 0.18) if shards else 1.0
    result = jax.random.normal(rng, extent, jnp.float32) * width * level
    return jnp.minimum(jnp.maximum(result, -most), most).astype(held_as)


def setup_inputs(seed: int = 0) -> dict:
    arg_keys = jax.random.split(jax.random.key(seed), 9)
    return {
        "layer_input": draw_layer_input(jax.random.fold_in(arg_keys[8], 71), 0),
        "caption_ids": draw_caption_ids(jax.random.fold_in(arg_keys[8], 71), 0),
        "positives": draw_positives(jax.random.fold_in(arg_keys[8], 71), 0),
        "ln_gain": jnp.clip(1.0 + 0.18 * jax.random.normal(arg_keys[3], (2, D), jnp.float32), 0.1, 1.9),
        "w_first": normal_values(arg_keys[4], (2, D, FFW), D ** -0.5, 0.1875, ((2, 8),)),
        "w_second": normal_values(arg_keys[5], (2, FFW, D), FFW ** -0.5, 0.125, ((1, 8),)),
        "logit_scale": jnp.clip(jnp.exp(jax.random.uniform(arg_keys[6], (1,), jnp.float32, math.log(20.0), math.log(80.0))), 20.0, 80.0),
        "logit_bias": jnp.clip(jax.random.uniform(arg_keys[7], (1,), jnp.float32, -6.0, -2.0), -6.0, -2.0),
    }


norm_eps = 1e-06
loss_scale = 128.0
gelu_coeff = 0.7978845608028654

def gelu_pair(pre):
    inner = gelu_coeff * (pre + 0.044715 * pre * pre * pre)
    tanh_part = jnp.tanh(inner)
    value = 0.5 * pre * (1.0 + tanh_part)
    slope = 0.5 * (1.0 + tanh_part) + 0.5 * pre * (1.0 - tanh_part * tanh_part) * gelu_coeff * (1.0 + 3.0 * 0.044715 * pre * pre)
    return (value, slope)

def normalize_rows(rows, gain):
    values = rows.astype(jnp.float32)
    centered = values - lax.optimization_barrier(jnp.mean(values, axis=-1, keepdims=True))
    variance = lax.optimization_barrier(jnp.mean(centered * centered, axis=-1, keepdims=True))
    inv_std = lax.rsqrt(variance + norm_eps)
    standard = centered * inv_std
    normed = (standard * gain).astype(jnp.bfloat16)
    return (values, standard, inv_std, normed)

def block_forward(rows, gain, first, second):
    values, standard, inv_std, normed = normalize_rows(rows, gain)
    pre = jnp.dot(normed, first, preferred_element_type=jnp.float32)
    value, slope = gelu_pair(pre)
    hidden = value.astype(jnp.bfloat16)
    block_out = values + jnp.dot(hidden, second, preferred_element_type=jnp.float32)
    return (block_out, standard, inv_std, slope)

def block_backward(grad_out, standard, inv_std, slope, gain, first, second):
    grad_rows = grad_out.astype(jnp.bfloat16)
    grad_hidden = jnp.dot(grad_rows, second.T, preferred_element_type=jnp.float32)
    grad_pre = (grad_hidden * slope).astype(jnp.bfloat16)
    grad_normed = jnp.dot(grad_pre, first.T, preferred_element_type=jnp.float32)
    grad_std = grad_normed * gain
    first_mean = lax.optimization_barrier(jnp.mean(grad_std, axis=-1, keepdims=True))
    second_mean = lax.optimization_barrier(jnp.mean(grad_std * standard, axis=-1, keepdims=True))
    return grad_out + inv_std * (grad_std - first_mean - standard * second_mean)

def unit_rows(pooled):
    norm = jnp.sqrt(lax.optimization_barrier(jnp.sum(pooled * pooled, axis=-1, keepdims=True)) + norm_eps)
    return (pooled / norm, norm)

def unit_back(unit, norm, grad_emb):
    return (grad_emb - unit * lax.optimization_barrier(jnp.sum(unit * grad_emb, axis=-1, keepdims=True))) / norm

def pool_image(block_out):
    return lax.optimization_barrier(jnp.mean(block_out.reshape(IMG_DEV, PATCHES, D), axis=1))

def pool_text(block_out, mask):
    counts = lax.optimization_barrier(jnp.sum(mask, axis=1, keepdims=True))
    summed = lax.optimization_barrier(jnp.sum(block_out.reshape(CAP_DEV, TEXT_LEN, D) * mask[:, :, None], axis=1))
    return summed / counts

def spread_image(grad_pooled):
    rows = jnp.broadcast_to(grad_pooled[:, None, :] / PATCHES, (IMG_DEV, PATCHES, D))
    return rows.reshape(ROWS, D)

def spread_text(grad_pooled, mask):
    counts = lax.optimization_barrier(jnp.sum(mask, axis=1, keepdims=True))
    rows = grad_pooled[:, None, :] * (mask / counts)[:, :, None]
    return rows.reshape(ROWS, D)

def reference(layer_input, caption_ids, positives, ln_gain, w_first, w_second, logit_scale, logit_bias):
    blocks = layer_input.reshape(N_BLK, N_TOWER, ROWS, D)
    image_blocks = blocks[:, :N_TOWER - 1].reshape(N_BLK * (N_TOWER - 1), ROWS, D)
    text_blocks = blocks[:, N_TOWER - 1]
    masks = (caption_ids != 0).astype(jnp.float32).reshape(N_BLK, CAP_DEV, TEXT_LEN)

    def image_embed(rows):
        block_out, standard, inv_std, slope = block_forward(rows, ln_gain[0], w_first[0], w_second[0])
        return pool_image(block_out)

    def text_embed(pair):
        rows, mask = pair
        block_out, standard, inv_std, slope = block_forward(rows, ln_gain[1], w_first[1], w_second[1])
        return pool_text(block_out, mask)
    image_pool = lax.map(image_embed, image_blocks).reshape(IMAGES, D)
    text_pool = lax.map(text_embed, (text_blocks, masks)).reshape(CAPTIONS, D)
    image_unit, image_norm = unit_rows(image_pool)
    text_unit, text_norm = unit_rows(text_pool)
    image_emb = image_unit.astype(jnp.bfloat16)
    text_emb = text_unit.astype(jnp.bfloat16)
    scale = logit_scale[0]
    bias = logit_bias[0]
    logits = scale * jnp.dot(image_emb, text_emb.T, preferred_element_type=jnp.float32) + bias
    onehot = (positives[:, None] == jnp.arange(CAPTIONS, dtype=jnp.int32)[None, :]).astype(jnp.float32)
    coef = (loss_scale * (jax.nn.sigmoid(logits) - onehot)).astype(jnp.bfloat16)
    grad_image = scale * jnp.dot(coef, text_emb, preferred_element_type=jnp.float32)
    grad_text = scale * jnp.dot(coef.T, image_emb, preferred_element_type=jnp.float32)
    image_gp = unit_back(image_unit, image_norm, grad_image).reshape(N_BLK * (N_TOWER - 1), IMG_DEV, D)
    text_gp = unit_back(text_unit, text_norm, grad_text).reshape(N_BLK, CAP_DEV, D)

    def image_back(pair):
        rows, grad_pooled = pair
        block_out, standard, inv_std, slope = block_forward(rows, ln_gain[0], w_first[0], w_second[0])
        grad_out = spread_image(grad_pooled)
        return block_backward(grad_out, standard, inv_std, slope, ln_gain[0], w_first[0], w_second[0])

    def text_back(triple):
        rows, grad_pooled, mask = triple
        block_out, standard, inv_std, slope = block_forward(rows, ln_gain[1], w_first[1], w_second[1])
        grad_out = spread_text(grad_pooled, mask)
        return block_backward(grad_out, standard, inv_std, slope, ln_gain[1], w_first[1], w_second[1])
    image_grads = lax.map(image_back, (image_blocks, image_gp)).reshape(N_BLK, N_TOWER - 1, ROWS, D)
    text_grads = lax.map(text_back, (text_blocks, text_gp, masks)).reshape(N_BLK, 1, ROWS, D)
    joined = jnp.concatenate([image_grads, text_grads], axis=1)
    return joined.reshape(N_BLK * N_TOWER * ROWS, D)
```

```python
import functools

import jax
import jax.numpy as jnp
from jax import lax
from jax.experimental import pallas as pl
from jax.experimental.pallas import tpu as pltpu
from jax.sharding import PartitionSpec as P

PATCHES = 256
TEXT_LEN = 64

norm_eps = 1e-06
loss_scale = 128.0
gelu_coeff = 0.7978845608028654


def gelu_pair(pre):
    inner = gelu_coeff * (pre + 0.044715 * pre * pre * pre)
    tanh_part = jnp.tanh(inner)
    value = 0.5 * pre * (1.0 + tanh_part)
    slope = 0.5 * (1.0 + tanh_part) + 0.5 * pre * (1.0 - tanh_part * tanh_part) * gelu_coeff * (
        1.0 + 3.0 * 0.044715 * pre * pre
    )
    return (value, slope)


def contract_last(left, right):
    return lax.dot_general(
        left, right, (((1,), (1,)), ((), ())), preferred_element_type=jnp.float32
    )


def two_parts(value):
    high = value.astype(jnp.bfloat16)
    low = (value - high.astype(jnp.float32)).astype(jnp.bfloat16)
    return high, low


def ring_place(block):
    return block // 2 if block % 2 == 0 else 7 - block // 2


RING = sorted(range(8), key=ring_place)


def ring_gather(own, groups):
    def move(value, step):
        found = []
        for place in range(8):
            for t in range(groups):
                source = RING[place] * groups + t
                found.append((source, RING[(place + step) % 8] * groups + t))
        return lax.ppermute(value, ("blk", "tower"), found)

    pieces = [[None, None] for _ in range(8)]
    pieces[0] = own
    for k in range(1, 5):
        for step in (1, -1):
            for chunk in (0, 1):
                if k == 4 and chunk != (0 if step == 1 else 1):
                    continue
                held = pieces[(-step * (k - 1)) % 8][chunk]
                pieces[(-step * k) % 8][chunk] = move(held, step)
    return pieces


SMALL = 128
REST = 16


def groups_of(pieces):
    found = [([(0, 0), (0, 1)], [0])]
    for k in (1, 2, 3):
        found.append(([(8 - k, 0), (k, 0)], []))
        found.append(([(8 - k, 1), (k, 1)], [8 - k, k]))
    found.append(([(4, 0), (4, 1)], [4]))
    return [(parts, rest, [pieces[p][c] for p, c in parts]) for parts, rest in found]


def project(rest, normed, one, two):
    weights = [one[:SMALL], two[:SMALL]]
    if rest:
        weights += [ref[SMALL:] for ref in (one, two) if ref.shape[0] > SMALL]
    pre = contract_last(normed[...], jnp.concatenate(weights, axis=0))
    square = pre * pre
    tanh_part = jnp.tanh(pre * (gelu_coeff + (gelu_coeff * 0.044715) * square))
    return pre, square, tanh_part, 0.5 + 0.5 * tanh_part


def slope_of(pre, square, tanh_part, gate, mask):
    bend = (0.5 * gelu_coeff) + (0.5 * gelu_coeff * 3.0 * 0.044715) * square
    slope = gate + pre * (1.0 - tanh_part * tanh_part) * bend
    return (slope * mask[...]).astype(jnp.bfloat16)


def pool_of(member, pre, gate):
    hidden = (pre * gate).astype(jnp.bfloat16)
    return jnp.dot(member[...], hidden, preferred_element_type=jnp.float32)


def put_pool(held, block_of, parts, rest, pool):
    for k, (p, c) in enumerate(parts):
        held[block_of[p], :, c * SMALL : (c + 1) * SMALL] = pool[:, k * SMALL : (k + 1) * SMALL]
    for k, p in enumerate(rest):
        start = 2 * SMALL + k * REST
        held[block_of[p], :, 2 * SMALL :] = pool[:, start : start + REST]


def own_kernel(
    parts, rest, block_of, layer_input, share, member, mask, normed, one, two, slope_ref, held, value
):
    pre, square, tanh_part, gate = project(rest, normed, one, two)
    slope = slope_of(pre, square, tanh_part, gate, mask)
    slope_ref[:, : slope.shape[1]] = slope
    held[...] = jnp.zeros_like(held)
    put_pool(held, block_of, parts, rest, pool_of(member, pre, gate) * share[...])
    value[...] = jnp.dot(member[...], layer_input[...], preferred_element_type=jnp.float32)


def forward_kernel(
    parts, rest, block_of, before, share, member, mask, normed, one, two, slope_ref, held
):
    pre, square, tanh_part, gate = project(rest, normed, one, two)
    slope = slope_of(pre, square, tanh_part, gate, mask)
    slope_ref[:, : slope.shape[1]] = slope
    held[...] = before[...]
    put_pool(held, block_of, parts, rest, pool_of(member, pre, gate) * share[...])


def pool_kernel(parts, rest, block_of, before, share, member, normed, one, two, held):
    pre, _, _, gate = project(rest, normed, one, two)
    held[...] = before[...]
    put_pool(held, block_of, parts, rest, pool_of(member, pre, gate) * share[...])


def last_pool_kernel(rest, share, member, normed, one, two, pool_ref):
    pre, _, _, gate = project(rest, normed, one, two)
    pool_ref[...] = pool_of(member, pre, gate) * share[...]


def late_slope_kernel(rests, mask, normed, *refs):
    count = len(rests)
    weights, slopes = refs[: 2 * count], refs[2 * count + 1 :]
    for k, rest in enumerate(rests):
        slope = slope_of(*project(rest, normed, weights[2 * k], weights[2 * k + 1]), mask)
        slopes[k][:, : slope.shape[1]] = slope


def backward_kernel(
    plan, flags, block_of, grad_hidden, own_row, gain, mask, layer_input, *refs
):
    count = len(plan)
    slopes = refs[:count]
    weight_refs = refs[count : 3 * count]
    out = refs[3 * count]
    is_text = flags[0] == 1
    step = pl.program_id(0)
    tile = layer_input.shape[0]
    bands = [pl.ds(k * TEXT_LEN, TEXT_LEN) for k in range(tile // TEXT_LEN)]
    slots = [
        jnp.where(
            is_text,
            step * len(bands) + k,
            flags[1] + (step * len(bands) + k) * TEXT_LEN // PATCHES,
        )
        for k in range(len(bands))
    ]
    def pick(lines, slot):
        row = lax.broadcasted_iota(jnp.int32, lines.shape, 0)
        return jnp.sum(jnp.where(row == slot, lines, 0.0), axis=0, keepdims=True)

    def scaled(slope_ref, start, lines):
        found = []
        for band, slot in zip(bands, slots):
            slope = slope_ref[band, start : start + lines.shape[1]].astype(jnp.float32)
            found.append((pick(lines, slot) * slope).astype(jnp.bfloat16))
        return jnp.concatenate(found, axis=0)

    def multiply(left, parts):
        right = jnp.concatenate(parts, axis=0)
        return jnp.dot(left, right, preferred_element_type=jnp.float32)

    def main_part(g):
        parts, _ = plan[g]
        lines = [grad_hidden[block_of[p], :, c * SMALL : (c + 1) * SMALL] for p, c in parts]
        return scaled(slopes[g], 0, jnp.concatenate(lines, axis=1))

    def rest_part(g):
        _, rest = plan[g]
        lines = [grad_hidden[block_of[p], :, 2 * SMALL :] for p in rest]
        return scaled(slopes[g], 2 * SMALL, jnp.concatenate(lines, axis=1))

    rests = [rest_part(g) for g in range(count) if plan[g][1]]
    total = None
    for g in range(0, count, 2):
        left = jnp.concatenate([main_part(g), main_part(g + 1)], axis=1)
        product = multiply(left, [ref[:SMALL] for ref in weight_refs[2 * g : 2 * g + 4]])
        total = product if total is None else total + product
    tails = [ref[SMALL:] for ref in weight_refs if ref.shape[0] > SMALL]
    total = total + multiply(jnp.concatenate(rests, axis=1), tails)

    values = layer_input[...].astype(jnp.float32)
    centered = values - jnp.mean(values, axis=-1, keepdims=True)
    variance = jnp.mean(centered * centered, axis=-1, keepdims=True)
    inv_std = lax.rsqrt(variance + norm_eps)
    standard = centered * inv_std
    grad_std = total * gain[...]
    first_mean = jnp.mean(grad_std, axis=-1, keepdims=True)
    second_mean = jnp.mean(grad_std * standard, axis=-1, keepdims=True)
    result = inv_std * (grad_std - first_mean - standard * second_mean)
    for k, (band, slot) in enumerate(zip(bands, slots)):
        grad_out = pick(own_row[...], slot) * mask[band, :]
        out[band, :] = grad_out + result[k * TEXT_LEN : (k + 1) * TEXT_LEN]


def backward_call(flags, block_of, grad_hidden, own_row, mask, layer_input, gain, slopes, groups):
    row_count, width = layer_input.shape
    tile = 2 * TEXT_LEN
    whole = pl.BlockSpec(memory_space=pltpu.VMEM)
    scalar = pl.BlockSpec(memory_space=pltpu.SMEM)

    def by_rows(cols):
        return pl.BlockSpec((tile, cols), lambda i: (i, 0))

    plan = [(parts, rest) for parts, rest, _ in groups]
    weights = [w for _, _, pair in groups for w in pair]
    count = len(plan)
    units = sum(w.shape[0] for w in weights)
    return pl.pallas_call(
        functools.partial(backward_kernel, plan),
        grid=(row_count // tile,),
        in_specs=[scalar] * 2
        + [whole] * 3
        + [by_rows(1), by_rows(width)]
        + [by_rows(slope.shape[1]) for slope in slopes]
        + [whole] * (2 * count),
        out_specs=by_rows(width),
        out_shape=jax.ShapeDtypeStruct((row_count, width), jnp.float32),
        compiler_params=pltpu.CompilerParams(vmem_limit_bytes=60 * 1024 * 1024),
        cost_estimate=pl.CostEstimate(
            flops=2 * row_count * width * units, bytes_accessed=12_000_000, transcendentals=0
        ),
    )(
        flags,
        block_of,
        grad_hidden,
        own_row,
        gain.reshape(1, width),
        mask,
        layer_input,
        *slopes,
        *weights,
    )


def partial_kernel(flags, block_of, share, value_pool, mine, late, w_second, out, pools, rows):
    slots, shard = late.shape
    pools[...] = mine[...]
    pools[block_of[4]] = late[...]
    high, low = two_parts(pools[...].reshape(8 * slots, shard))
    second = w_second[flags[0]]
    both = jnp.dot(
        jnp.concatenate([high, low], axis=0), second, preferred_element_type=jnp.float32
    )
    rows[...] = both[: 8 * slots] + both[8 * slots :]
    own = pl.ds(pl.multiple_of(flags[2] * slots, slots), slots)
    rows[own, :] += value_pool[...] * share[...]
    pair = out.shape[1]
    for k in range(out.shape[0]):
        out[k] = rows[k * pair : (k + 1) * pair, :].astype(out.dtype)


def embed_kernel(groups, notes, back, *refs):
    out = refs[-1]

    def total(places):
        found = back[places[0]].astype(jnp.float32)
        for place in places[1:]:
            found = found + back[place].astype(jnp.float32)
        return found

    devices = range(back.shape[0])
    image = total([d for d in devices if d % groups < groups - 1])
    text = total([d for d in devices if d % groups == groups - 1])
    pooled = jnp.concatenate([image, text], axis=0)
    norm = jnp.sqrt(jnp.sum(pooled * pooled, axis=-1, keepdims=True) + norm_eps)
    emb = (pooled / norm).astype(jnp.bfloat16)
    high = norm.astype(jnp.bfloat16).astype(jnp.float32)
    lane = lax.broadcasted_iota(jnp.int32, notes.shape, 1)
    marks = jnp.where(lane == 0, high, jnp.where(lane == 1, norm - high, notes[...]))
    row = jnp.concatenate([emb, marks.astype(jnp.bfloat16)], axis=1)
    out[...] = jnp.broadcast_to(row[None], out.shape)


def loss_kernel(groups, flags, scalars, packed, w_second, grad_cols, own_row, rows_ref):
    is_text = flags[0] == 1
    scale, bias = scalars[0], scalars[1]
    count, total_width = packed.shape
    width = own_row.shape[1]
    half = count // 2
    row = lax.broadcasted_iota(jnp.int32, (half, count), 0)
    column = lax.broadcasted_iota(jnp.int32, (half, count), 1)
    place = 4 * (row // 2) + row % 2
    everything = packed[...]

    def chosen(offset):
        which = (column == place + offset).astype(jnp.bfloat16)
        return jnp.dot(which, everything, preferred_element_type=jnp.float32)

    image, text = chosen(0), chosen(2)
    image16 = image[:, :width].astype(jnp.bfloat16)
    text16 = text[:, :width].astype(jnp.bfloat16)
    logits = scale * contract_last(image16, text16) + bias
    positive = image[:, width + 2 : width + 3] * 64.0 + image[:, width + 3 : width + 4]
    row = lax.broadcasted_iota(jnp.int32, (half, half), 0)
    column = lax.broadcasted_iota(jnp.int32, (half, half), 1)
    onehot = (column.astype(jnp.float32) == positive).astype(jnp.float32)
    sigmoid = 1.0 / (1.0 + jnp.exp(-logits))
    real = row % (2 * groups) < 2 * (groups - 1)
    coef = jnp.where(real, loss_scale * (sigmoid - onehot), 0.0)
    left = jnp.where(is_text, coef.T, coef).astype(jnp.bfloat16)
    right = jnp.where(is_text, image16, text16)
    grad_emb = scale * jnp.dot(left, right, preferred_element_type=jnp.float32)
    own = jnp.where(is_text, text, image)
    unit = own[:, :width]
    norm = own[:, width : width + 1] + own[:, width + 1 : width + 2]
    rows = own[:, width + 4 : width + 5]
    grad_pooled = grad_emb - unit * jnp.sum(unit * grad_emb, axis=-1, keepdims=True)
    grad_row = grad_pooled / (norm * rows)
    rows_ref[...] = grad_row
    own_row[...] = rows_ref[pl.ds(pl.multiple_of(flags[2] * 8, 8), 8), :]
    second = w_second[flags[0]]
    columns = contract_last(grad_row.astype(jnp.bfloat16), second)
    for block in range(grad_cols.shape[0]):
        grad_cols[block] = columns[block * 8 : (block + 1) * 8]


def small_call(kernel, outs, operands, scalars, scratch=(), flops=0, moved=0, outside=0):
    single = not isinstance(outs, tuple)
    whole = pl.BlockSpec(memory_space=pltpu.VMEM)
    scalar = pl.BlockSpec(memory_space=pltpu.SMEM)
    return pl.pallas_call(
        kernel,
        in_specs=[scalar] * scalars
        + [whole] * (len(operands) - scalars - outside)
        + [pl.BlockSpec(memory_space=pl.ANY)] * outside,
        out_specs=whole if single else tuple(whole for _ in outs),
        out_shape=outs,
        scratch_shapes=scratch,
        compiler_params=pltpu.CompilerParams(vmem_limit_bytes=16 * 1024 * 1024),
        cost_estimate=pl.CostEstimate(flops=flops, bytes_accessed=moved, transcendentals=0),
    )(*operands)


def ring_body(
    layer_input, caption_ids, positives, ln_gain, w_first, w_second, logit_scale, logit_bias
):
    groups = lax.axis_size("tower")
    tower_index = lax.axis_index("tower")
    block_index = lax.axis_index("blk")
    is_text = tower_index == groups - 1
    row_count, width = layer_input.shape
    slots = caption_ids.shape[0]
    img_count = positives.shape[0] // (groups - 1)
    shard = w_first.shape[2]
    gain = jnp.where(is_text, ln_gain[1], ln_gain[0])
    own = [
        jnp.where(is_text, w_first[1, :, cut].T, w_first[0, :, cut].T)
        for cut in (slice(0, SMALL), slice(SMALL, shard))
    ]
    flags = jnp.stack([is_text.astype(jnp.int32), tower_index * img_count, block_index])
    flags = flags.astype(jnp.int32)
    place = jnp.where(block_index % 2 == 0, block_index // 2, 7 - block_index // 2)
    around = (place + jnp.arange(8, dtype=jnp.int32)) % 8
    block_of = jnp.where(around < 4, 2 * around, 2 * (7 - around) + 1).astype(jnp.int32)

    mask = (caption_ids != 0).astype(jnp.float32)
    counts = jnp.sum(mask, axis=1, keepdims=True)
    row = jnp.arange(row_count, dtype=jnp.int32)[None, :]
    slot = jnp.arange(slots, dtype=jnp.int32)[:, None]
    row_mask = jnp.where(is_text, mask.reshape(1, row_count), 1.0)
    slot_of = jnp.where(is_text, row // TEXT_LEN, tower_index * img_count + row // PATCHES)
    member16 = jnp.where(slot_of == slot, row_mask, 0.0).astype(jnp.bfloat16)
    share = jnp.where(is_text, 1.0 / counts, 1.0 / PATCHES)

    values = layer_input.astype(jnp.float32)
    centered = values - jnp.mean(values, axis=-1, keepdims=True)
    variance = jnp.mean(centered * centered, axis=-1, keepdims=True)
    normed = (centered * lax.rsqrt(variance + norm_eps) * gain).astype(jnp.bfloat16)
    row_mask = row_mask.reshape(row_count, 1)
    arrivals = groups_of(ring_gather(own, groups))
    plan = [(parts, rest) for parts, rest, _ in arrivals]
    share = share.astype(jnp.float32)
    cost = {"flops": int(4e9), "moved": int(16e6)}
    held_shape = jax.ShapeDtypeStruct((8, slots, shard), jnp.float32)
    slopes = []
    held = value_pool = last_pool = None
    for k, (parts, rest, (one, two)) in enumerate(arrivals):
        columns = 3 * SMALL if rest else 2 * SMALL
        slope_shape = jax.ShapeDtypeStruct((row_count, columns), jnp.bfloat16)
        shared = [share, member16]
        weights = [normed, one, two]
        if k == 0:
            slope, held, value_pool = small_call(
                functools.partial(own_kernel, parts, rest),
                (slope_shape, held_shape, jax.ShapeDtypeStruct((slots, width), jnp.float32)),
                [block_of, layer_input, *shared, row_mask, *weights],
                1,
                **cost,
            )
            slopes.append(slope)
        elif k < len(arrivals) - 2:
            slope, held = small_call(
                functools.partial(forward_kernel, parts, rest),
                (slope_shape, held_shape),
                [block_of, held, *shared, row_mask, *weights],
                1,
                **cost,
            )
            slopes.append(slope)
        elif k == len(arrivals) - 2:
            held = small_call(
                functools.partial(pool_kernel, parts, rest),
                held_shape,
                [block_of, held, *shared, *weights],
                1,
                **cost,
            )
        else:
            last_pool = small_call(
                functools.partial(last_pool_kernel, rest),
                jax.ShapeDtypeStruct((slots, shard), jnp.float32),
                [*shared, *weights],
                0,
                **cost,
            )

    devices = 8 * groups
    pair = slots // groups
    mine = lax.all_to_all(held, "blk", 0, 0)
    opposite = []
    for place in range(8):
        for t in range(groups):
            source = RING[place] * groups + t
            opposite.append((source, RING[(place + 4) % 8] * groups + t))
    late = lax.ppermute(last_pool, ("blk", "tower"), opposite)
    partial = small_call(
        partial_kernel,
        jax.ShapeDtypeStruct((devices, pair, width), jnp.bfloat16),
        [flags, block_of, share, value_pool, mine, late, w_second],
        2,
        (
            pltpu.VMEM((8, slots, shard), jnp.float32),
            pltpu.VMEM((8 * slots, width), jnp.float32),
        ),
    )
    back = lax.all_to_all(partial, ("blk", "tower"), 0, 0)
    slopes += small_call(
        functools.partial(late_slope_kernel, [rest for _, rest, _ in arrivals[-2:]]),
        (jax.ShapeDtypeStruct((row_count, 3 * SMALL), jnp.bfloat16),) * 2,
        [row_mask, normed] + [w for _, _, pair_of in arrivals[-2:] for w in pair_of] + [partial],
        0,
        flops=int(1e9),
        moved=int(4e6),
        outside=1,
    )

    start = jnp.minimum(tower_index, groups - 2) * img_count
    own_positive = lax.dynamic_slice_in_dim(positives, start, img_count, 0)
    own_counts = lax.dynamic_slice_in_dim(counts[:, 0], tower_index * pair, pair, 0)
    none = jnp.zeros((pair,), jnp.int32)
    notes = jnp.stack(
        [
            jnp.zeros((2 * pair,), jnp.float32),
            jnp.zeros((2 * pair,), jnp.float32),
            jnp.concatenate([own_positive // 64, none]).astype(jnp.float32),
            jnp.concatenate([own_positive % 64, none]).astype(jnp.float32),
            jnp.concatenate([jnp.full((pair,), PATCHES, jnp.float32), own_counts]),
        ],
        axis=1,
    )
    notes = jnp.pad(notes, ((0, 0), (0, 128 - notes.shape[1])))
    copies = small_call(
        functools.partial(embed_kernel, groups),
        jax.ShapeDtypeStruct((devices, 2 * pair, width + 128), jnp.bfloat16),
        [notes, back, *slopes[-2:]],
        0,
        outside=2,
    )
    packed = lax.all_to_all(copies, ("blk", "tower"), 0, 0)
    packed = packed.reshape(devices * 2 * pair, width + 128)
    grad_cols, own_row = small_call(
        functools.partial(loss_kernel, groups),
        (
            jax.ShapeDtypeStruct((8, slots, shard), jnp.float32),
            jax.ShapeDtypeStruct((slots, width), jnp.float32),
        ),
        [flags, jnp.concatenate([logit_scale, logit_bias]), packed, w_second],
        2,
        (pltpu.VMEM((devices * pair, width), jnp.float32),),
    )
    grad_hidden = lax.all_to_all(grad_cols, "blk", 0, 0)
    return backward_call(
        flags,
        block_of,
        grad_hidden,
        own_row,
        row_mask,
        layer_input,
        gain,
        slopes,
        arrivals,
    )


def general_body(layer_input, caption_ids, positives, ln_gain, w_first, w_second, logit_scale, logit_bias):
    groups = lax.axis_size("tower")
    blocks = lax.axis_size("blk")
    tower_index = lax.axis_index("tower")
    block_index = lax.axis_index("blk")
    is_text = tower_index == groups - 1
    row_count, width = layer_input.shape
    slots = caption_ids.shape[0]
    img_count = positives.shape[0] // (groups - 1)
    shard = w_first.shape[2]
    gain = jnp.where(is_text, ln_gain[1], ln_gain[0])
    first = jnp.where(is_text, w_first[1].T, w_first[0].T)
    second = jnp.where(is_text, w_second[1], w_second[0])

    mask = (caption_ids != 0).astype(jnp.float32)
    counts = jnp.sum(mask, axis=1, keepdims=True)
    row = jnp.arange(row_count, dtype=jnp.int32)[None, :]
    slot = jnp.arange(slots, dtype=jnp.int32)[:, None]
    row_mask = jnp.where(is_text, mask.reshape(1, row_count), 1.0)
    member = jnp.where(jnp.where(is_text, row // TEXT_LEN, row // PATCHES) == slot, row_mask, 0.0)
    share = jnp.where(is_text, 1.0 / counts, 1.0 / PATCHES)
    member16 = member.astype(jnp.bfloat16)

    values = layer_input.astype(jnp.float32)
    centered = values - jnp.mean(values, axis=-1, keepdims=True)
    variance = jnp.mean(centered * centered, axis=-1, keepdims=True)
    inv_std = lax.rsqrt(variance + norm_eps)
    standard = centered * inv_std
    normed = (standard * gain).astype(jnp.bfloat16)
    full = lax.all_gather(first, "blk", axis=0, tiled=True)
    value, slope = gelu_pair(contract_last(normed, full))
    hidden_pool = jnp.dot(member16, value.astype(jnp.bfloat16), preferred_element_type=jnp.float32)
    hidden_pool = hidden_pool * share
    value_pool = jnp.dot(member16, layer_input, preferred_element_type=jnp.float32) * share

    sent = hidden_pool.reshape(slots, blocks, shard).transpose(1, 0, 2)
    mine = lax.all_to_all(sent, "blk", 0, 0).reshape(blocks * slots, shard)
    high, low = two_parts(mine)
    partial = jnp.dot(high, second, preferred_element_type=jnp.float32) + jnp.dot(
        low, second, preferred_element_type=jnp.float32
    )
    back = lax.all_to_all(partial.reshape(blocks, slots, width), "blk", 0, 0)
    pooled = value_pool + jnp.sum(back, axis=0)

    norm = jnp.sqrt(jnp.sum(pooled * pooled, axis=-1, keepdims=True) + norm_eps)
    emb = (pooled / norm).astype(jnp.bfloat16)
    norm_high, norm_low = two_parts(norm)
    start = jnp.minimum(tower_index, groups - 2) * img_count
    own_positive = lax.dynamic_slice_in_dim(positives, start, img_count, 0)
    own_positive = jnp.pad(own_positive, (0, slots - img_count))[:, None]
    extra = jnp.concatenate(
        [
            norm_high,
            norm_low,
            (own_positive // 64).astype(jnp.bfloat16),
            (own_positive % 64).astype(jnp.bfloat16),
            jnp.where(is_text, counts, PATCHES).astype(jnp.bfloat16),
        ],
        axis=1,
    )
    extra = jnp.pad(extra, ((0, 0), (0, 128 - extra.shape[1])))
    packed = jnp.concatenate([emb, extra], axis=1)
    packed = lax.all_to_all(
        jnp.broadcast_to(packed[None], (groups * blocks, *packed.shape)), ("tower", "blk"), 0, 0
    ).reshape(groups * blocks * slots, packed.shape[1])
    every = packed[:, :width]
    notes = packed[:, width : width + 5].astype(jnp.float32)
    every_norm = notes[:, :1] + notes[:, 1:2]
    every_positive = (notes[:, 2:3] * 64.0 + notes[:, 3:4]).astype(jnp.int32)

    scale = logit_scale[0]
    bias = logit_bias[0]
    images = (groups - 1) * blocks * slots
    column = blocks * slots
    text_emb = every[images:]
    logits = scale * contract_last(every[:images], text_emb) + bias
    caption_index = jnp.arange(column, dtype=jnp.int32)[None, :]
    onehot = (every_positive[:images] == caption_index).astype(jnp.float32)
    real = (jnp.arange(images, dtype=jnp.int32) % slots < img_count)[:, None]
    coef = jnp.where(real, loss_scale * (jax.nn.sigmoid(logits) - onehot), 0.0).astype(jnp.bfloat16)
    own = lax.dynamic_slice_in_dim(every, tower_index * column, column, 0)
    own_norm = lax.dynamic_slice_in_dim(every_norm, tower_index * column, column, 0)
    own_coef = lax.dynamic_slice_in_dim(coef, jnp.minimum(tower_index, groups - 2) * column, column, 0)
    grad_image = jnp.dot(own_coef, text_emb, preferred_element_type=jnp.float32)
    grad_text = lax.dot_general(
        coef, every[:images], (((0,), (0,)), ((), ())), preferred_element_type=jnp.float32
    )
    grad_emb = scale * jnp.where(is_text, grad_text, grad_image)
    unit = own.astype(jnp.float32)
    grad_pooled = (grad_emb - unit * jnp.sum(unit * grad_emb, axis=-1, keepdims=True)) / own_norm
    own_rows = lax.dynamic_slice_in_dim(notes[:, 4:5], tower_index * column, column, 0)
    grad_row = grad_pooled / own_rows
    grad_cols = contract_last(grad_row.astype(jnp.bfloat16), second)
    grad_hidden = lax.all_to_all(grad_cols.reshape(blocks, slots, shard), "blk", 0, 0)
    own_row = lax.dynamic_slice_in_dim(grad_row, block_index * slots, slots, 0)
    def spread(rows):
        cols = rows.shape[1]
        image = jnp.broadcast_to(
            rows[:img_count, None, :], (img_count, PATCHES, cols)
        ).reshape(row_count, cols)
        text = (rows[:, None, :] * mask[:, :, None]).reshape(row_count, cols)
        return jnp.where(is_text, text, image)

    grad_hidden = grad_hidden.transpose(1, 0, 2).reshape(slots, blocks * shard)
    grad_out = spread(own_row)
    grad_pre = (spread(grad_hidden) * slope).astype(jnp.bfloat16)
    grad_normed = jnp.dot(grad_pre, full, preferred_element_type=jnp.float32)
    grad_std = grad_normed * gain
    first_mean = jnp.mean(grad_std, axis=-1, keepdims=True)
    second_mean = jnp.mean(grad_std * standard, axis=-1, keepdims=True)
    return grad_out + inv_std * (grad_std - first_mean - standard * second_mean)


def body(layer_input, *others):
    w_first = others[3]
    ring = (
        lax.axis_size("blk") == 8
        and lax.axis_size("tower") == 4
        and w_first.shape[2] == 272
        and others[0].shape[0] == 8
        and others[1].shape[0] == 6
    )
    return (ring_body if ring else general_body)(layer_input, *others)


def solution(mesh):
    placed = (
        P(("blk", "tower"), None),
        P("blk", None),
        P("blk"),
        P(),
        P(None, None, "blk"),
        P(None, "blk", None),
        P(),
        P(),
    )
    return jax.shard_map(
        body, mesh=mesh, in_specs=placed, out_specs=P(("blk", "tower"), None), check_vma=False
    )
```

```python
import functools

import jax
import jax.numpy as jnp
from jax import lax
from jax.experimental import pallas as pl
from jax.experimental.pallas import tpu as pltpu
from jax.sharding import PartitionSpec as P

PATCHES = 256
TEXT_LEN = 64

norm_eps = 1e-06
loss_scale = 128.0
gelu_coeff = 0.7978845608028654


def gelu_pair(pre):
    inner = gelu_coeff * (pre + 0.044715 * pre * pre * pre)
    tanh_part = jnp.tanh(inner)
    value = 0.5 * pre * (1.0 + tanh_part)
    slope = 0.5 * (1.0 + tanh_part) + 0.5 * pre * (1.0 - tanh_part * tanh_part) * gelu_coeff * (
        1.0 + 3.0 * 0.044715 * pre * pre
    )
    return (value, slope)


def contract_last(left, right):
    return lax.dot_general(
        left, right, (((1,), (1,)), ((), ())), preferred_element_type=jnp.float32
    )


def two_parts(value):
    high = value.astype(jnp.bfloat16)
    low = (value - high.astype(jnp.float32)).astype(jnp.bfloat16)
    return high, low


def ring_place(block):
    return block // 2 if block % 2 == 0 else 7 - block // 2


RING = sorted(range(8), key=ring_place)


def ring_gather(own, groups):
    def move(value, step):
        found = []
        for place in range(8):
            for t in range(groups):
                source = RING[place] * groups + t
                found.append((source, RING[(place + step) % 8] * groups + t))
        return lax.ppermute(value, ("blk", "tower"), found)

    pieces = [[None, None] for _ in range(8)]
    pieces[0] = own
    for k in range(1, 5):
        for step in (1, -1):
            for chunk in (0, 1):
                if k == 4 and chunk != (0 if step == 1 else 1):
                    continue
                held = pieces[(-step * (k - 1)) % 8][chunk]
                pieces[(-step * k) % 8][chunk] = move(held, step)
    return pieces


SMALL = 128
REST = 16


def groups_of(pieces):
    found = [([(0, 0), (0, 1)], [0])]
    for k in (1, 2, 3):
        found.append(([(8 - k, 0), (k, 0)], []))
        found.append(([(8 - k, 1), (k, 1)], [8 - k, k]))
    found.append(([(4, 0), (4, 1)], [4]))
    return [(parts, rest, [pieces[p][c] for p, c in parts]) for parts, rest in found]


def project(rest, normed, one, two):
    weights = [one[:SMALL], two[:SMALL]]
    if rest:
        weights += [ref[SMALL:] for ref in (one, two) if ref.shape[0] > SMALL]
    pre = contract_last(normed[...], jnp.concatenate(weights, axis=0))
    square = pre * pre
    tanh_part = jnp.tanh(pre * (gelu_coeff + (gelu_coeff * 0.044715) * square))
    return pre, square, tanh_part, 0.5 + 0.5 * tanh_part


def slope_of(pre, square, tanh_part, gate, mask):
    bend = (0.5 * gelu_coeff) + (0.5 * gelu_coeff * 3.0 * 0.044715) * square
    slope = gate + pre * (1.0 - tanh_part * tanh_part) * bend
    return (slope * mask[...]).astype(jnp.bfloat16)


def pool_of(member, pre, gate):
    hidden = (pre * gate).astype(jnp.bfloat16)
    return jnp.dot(member[...], hidden, preferred_element_type=jnp.float32)


def put_pool(held, block_of, parts, rest, pool):
    for k, (p, c) in enumerate(parts):
        held[block_of[p], :, c * SMALL : (c + 1) * SMALL] = pool[:, k * SMALL : (k + 1) * SMALL]
    for k, p in enumerate(rest):
        start = 2 * SMALL + k * REST
        held[block_of[p], :, 2 * SMALL :] = pool[:, start : start + REST]


def own_kernel(
    parts, rest, block_of, layer_input, share, member, mask, normed, one, two, slope_ref, held, value
):
    pre, square, tanh_part, gate = project(rest, normed, one, two)
    slope = slope_of(pre, square, tanh_part, gate, mask)
    slope_ref[:, : slope.shape[1]] = slope
    held[...] = jnp.zeros_like(held)
    put_pool(held, block_of, parts, rest, pool_of(member, pre, gate) * share[...])
    value[...] = jnp.dot(member[...], layer_input[...], preferred_element_type=jnp.float32)


def forward_kernel(
    parts, rest, block_of, before, share, member, mask, normed, one, two, slope_ref, held
):
    pre, square, tanh_part, gate = project(rest, normed, one, two)
    slope = slope_of(pre, square, tanh_part, gate, mask)
    slope_ref[:, : slope.shape[1]] = slope
    held[...] = before[...]
    put_pool(held, block_of, parts, rest, pool_of(member, pre, gate) * share[...])


def last_pool_kernel(rest, share, member, normed, one, two, pool_ref):
    pre, _, _, gate = project(rest, normed, one, two)
    pool_ref[...] = pool_of(member, pre, gate) * share[...]


def late_slope_kernel(rest, mask, normed, one, two, after, slope_ref):
    slope = slope_of(*project(rest, normed, one, two), mask)
    slope_ref[:, : slope.shape[1]] = slope


def backward_kernel(
    plan, flags, block_of, grad_hidden, own_row, gain, mask, layer_input, *refs
):
    count = len(plan)
    slopes = refs[:count]
    weight_refs = refs[count : 3 * count]
    out = refs[3 * count]
    is_text = flags[0] == 1
    step = pl.program_id(0)
    tile = layer_input.shape[0]
    bands = [pl.ds(k * TEXT_LEN, TEXT_LEN) for k in range(tile // TEXT_LEN)]
    slots = [
        jnp.where(
            is_text,
            step * len(bands) + k,
            flags[1] + (step * len(bands) + k) * TEXT_LEN // PATCHES,
        )
        for k in range(len(bands))
    ]
    def pick(lines, slot):
        row = lax.broadcasted_iota(jnp.int32, lines.shape, 0)
        return jnp.sum(jnp.where(row == slot, lines, 0.0), axis=0, keepdims=True)

    def scaled(slope_ref, start, lines):
        found = []
        for band, slot in zip(bands, slots):
            slope = slope_ref[band, start : start + lines.shape[1]].astype(jnp.float32)
            found.append((pick(lines, slot) * slope).astype(jnp.bfloat16))
        return jnp.concatenate(found, axis=0)

    def multiply(left, parts):
        right = jnp.concatenate(parts, axis=0)
        return jnp.dot(left, right, preferred_element_type=jnp.float32)

    def main_part(g):
        parts, _ = plan[g]
        lines = [grad_hidden[block_of[p], :, c * SMALL : (c + 1) * SMALL] for p, c in parts]
        return scaled(slopes[g], 0, jnp.concatenate(lines, axis=1))

    def rest_part(g):
        _, rest = plan[g]
        lines = [grad_hidden[block_of[p], :, 2 * SMALL :] for p in rest]
        return scaled(slopes[g], 2 * SMALL, jnp.concatenate(lines, axis=1))

    rests = [rest_part(g) for g in range(count) if plan[g][1]]
    total = None
    for g in range(0, count, 2):
        left = jnp.concatenate([main_part(g), main_part(g + 1)], axis=1)
        product = multiply(left, [ref[:SMALL] for ref in weight_refs[2 * g : 2 * g + 4]])
        total = product if total is None else total + product
    tails = [ref[SMALL:] for ref in weight_refs if ref.shape[0] > SMALL]
    total = total + multiply(jnp.concatenate(rests, axis=1), tails)

    values = layer_input[...].astype(jnp.float32)
    centered = values - jnp.mean(values, axis=-1, keepdims=True)
    variance = jnp.mean(centered * centered, axis=-1, keepdims=True)
    inv_std = lax.rsqrt(variance + norm_eps)
    standard = centered * inv_std
    grad_std = total * gain[...]
    first_mean = jnp.mean(grad_std, axis=-1, keepdims=True)
    second_mean = jnp.mean(grad_std * standard, axis=-1, keepdims=True)
    result = inv_std * (grad_std - first_mean - standard * second_mean)
    for k, (band, slot) in enumerate(zip(bands, slots)):
        grad_out = pick(own_row[...], slot) * mask[band, :]
        out[band, :] = grad_out + result[k * TEXT_LEN : (k + 1) * TEXT_LEN]


def backward_call(flags, block_of, grad_hidden, own_row, mask, layer_input, gain, slopes, groups):
    row_count, width = layer_input.shape
    tile = 2 * TEXT_LEN
    whole = pl.BlockSpec(memory_space=pltpu.VMEM)
    scalar = pl.BlockSpec(memory_space=pltpu.SMEM)

    def by_rows(cols):
        return pl.BlockSpec((tile, cols), lambda i: (i, 0))

    plan = [(parts, rest) for parts, rest, _ in groups]
    weights = [w for _, _, pair in groups for w in pair]
    count = len(plan)
    units = sum(w.shape[0] for w in weights)
    return pl.pallas_call(
        functools.partial(backward_kernel, plan),
        grid=(row_count // tile,),
        in_specs=[scalar] * 2
        + [whole] * 3
        + [by_rows(1), by_rows(width)]
        + [by_rows(slope.shape[1]) for slope in slopes]
        + [whole] * (2 * count),
        out_specs=by_rows(width),
        out_shape=jax.ShapeDtypeStruct((row_count, width), jnp.float32),
        compiler_params=pltpu.CompilerParams(vmem_limit_bytes=60 * 1024 * 1024),
        cost_estimate=pl.CostEstimate(
            flops=2 * row_count * width * units, bytes_accessed=12_000_000, transcendentals=0
        ),
    )(
        flags,
        block_of,
        grad_hidden,
        own_row,
        gain.reshape(1, width),
        mask,
        layer_input,
        *slopes,
        *weights,
    )


def partial_kernel(flags, block_of, share, value_pool, mine, late, w_second, out, pools, rows):
    slots, shard = late.shape
    pools[...] = mine[...]
    pools[block_of[4]] = late[...]
    high, low = two_parts(pools[...].reshape(8 * slots, shard))
    second = w_second[flags[0]]
    both = jnp.dot(
        jnp.concatenate([high, low], axis=0), second, preferred_element_type=jnp.float32
    )
    rows[...] = both[: 8 * slots] + both[8 * slots :]
    own = pl.ds(pl.multiple_of(flags[2] * slots, slots), slots)
    rows[own, :] += value_pool[...] * share[...]
    pair = out.shape[1]
    for k in range(out.shape[0]):
        out[k] = rows[k * pair : (k + 1) * pair, :].astype(out.dtype)


def embed_kernel(groups, notes, back, *refs):
    out = refs[-1]

    def total(places):
        found = back[places[0]].astype(jnp.float32)
        for place in places[1:]:
            found = found + back[place].astype(jnp.float32)
        return found

    devices = range(back.shape[0])
    image = total([d for d in devices if d % groups < groups - 1])
    text = total([d for d in devices if d % groups == groups - 1])
    pooled = jnp.concatenate([image, text], axis=0)
    norm = jnp.sqrt(jnp.sum(pooled * pooled, axis=-1, keepdims=True) + norm_eps)
    emb = (pooled / norm).astype(jnp.bfloat16)
    high = norm.astype(jnp.bfloat16).astype(jnp.float32)
    lane = lax.broadcasted_iota(jnp.int32, notes.shape, 1)
    marks = jnp.where(lane == 0, high, jnp.where(lane == 1, norm - high, notes[...]))
    row = jnp.concatenate([emb, marks.astype(jnp.bfloat16)], axis=1)
    out[...] = jnp.broadcast_to(row[None], out.shape)


def loss_kernel(groups, flags, scalars, packed, w_second, grad_cols, own_row, rows_ref):
    is_text = flags[0] == 1
    scale, bias = scalars[0], scalars[1]
    count, total_width = packed.shape
    width = own_row.shape[1]
    half = count // 2
    row = lax.broadcasted_iota(jnp.int32, (half, count), 0)
    column = lax.broadcasted_iota(jnp.int32, (half, count), 1)
    place = 4 * (row // 2) + row % 2
    everything = packed[...]

    def chosen(offset):
        which = (column == place + offset).astype(jnp.bfloat16)
        return jnp.dot(which, everything, preferred_element_type=jnp.float32)

    image, text = chosen(0), chosen(2)
    image16 = image[:, :width].astype(jnp.bfloat16)
    text16 = text[:, :width].astype(jnp.bfloat16)
    logits = scale * contract_last(image16, text16) + bias
    positive = image[:, width + 2 : width + 3] * 64.0 + image[:, width + 3 : width + 4]
    row = lax.broadcasted_iota(jnp.int32, (half, half), 0)
    column = lax.broadcasted_iota(jnp.int32, (half, half), 1)
    onehot = (column.astype(jnp.float32) == positive).astype(jnp.float32)
    sigmoid = 1.0 / (1.0 + jnp.exp(-logits))
    real = row % (2 * groups) < 2 * (groups - 1)
    coef = jnp.where(real, loss_scale * (sigmoid - onehot), 0.0)
    left = jnp.where(is_text, coef.T, coef).astype(jnp.bfloat16)
    right = jnp.where(is_text, image16, text16)
    grad_emb = scale * jnp.dot(left, right, preferred_element_type=jnp.float32)
    own = jnp.where(is_text, text, image)
    unit = own[:, :width]
    norm = own[:, width : width + 1] + own[:, width + 1 : width + 2]
    rows = own[:, width + 4 : width + 5]
    grad_pooled = grad_emb - unit * jnp.sum(unit * grad_emb, axis=-1, keepdims=True)
    grad_row = grad_pooled / (norm * rows)
    rows_ref[...] = grad_row
    own_row[...] = rows_ref[pl.ds(pl.multiple_of(flags[2] * 8, 8), 8), :]
    second = w_second[flags[0]]
    columns = contract_last(grad_row.astype(jnp.bfloat16), second)
    for block in range(grad_cols.shape[0]):
        grad_cols[block] = columns[block * 8 : (block + 1) * 8]


def small_call(kernel, outs, operands, scalars, scratch=(), flops=0, moved=0, outside=0):
    single = not isinstance(outs, tuple)
    whole = pl.BlockSpec(memory_space=pltpu.VMEM)
    scalar = pl.BlockSpec(memory_space=pltpu.SMEM)
    return pl.pallas_call(
        kernel,
        in_specs=[scalar] * scalars
        + [whole] * (len(operands) - scalars - outside)
        + [pl.BlockSpec(memory_space=pl.ANY)] * outside,
        out_specs=whole if single else tuple(whole for _ in outs),
        out_shape=outs,
        scratch_shapes=scratch,
        compiler_params=pltpu.CompilerParams(vmem_limit_bytes=16 * 1024 * 1024),
        cost_estimate=pl.CostEstimate(flops=flops, bytes_accessed=moved, transcendentals=0),
    )(*operands)


def ring_body(
    layer_input, caption_ids, positives, ln_gain, w_first, w_second, logit_scale, logit_bias
):
    groups = lax.axis_size("tower")
    tower_index = lax.axis_index("tower")
    block_index = lax.axis_index("blk")
    is_text = tower_index == groups - 1
    row_count, width = layer_input.shape
    slots = caption_ids.shape[0]
    img_count = positives.shape[0] // (groups - 1)
    shard = w_first.shape[2]
    gain = jnp.where(is_text, ln_gain[1], ln_gain[0])
    own = [
        jnp.where(is_text, w_first[1, :, cut].T, w_first[0, :, cut].T)
        for cut in (slice(0, SMALL), slice(SMALL, shard))
    ]
    flags = jnp.stack([is_text.astype(jnp.int32), tower_index * img_count, block_index])
    flags = flags.astype(jnp.int32)
    place = jnp.where(block_index % 2 == 0, block_index // 2, 7 - block_index // 2)
    around = (place + jnp.arange(8, dtype=jnp.int32)) % 8
    block_of = jnp.where(around < 4, 2 * around, 2 * (7 - around) + 1).astype(jnp.int32)

    mask = (caption_ids != 0).astype(jnp.float32)
    counts = jnp.sum(mask, axis=1, keepdims=True)
    row = jnp.arange(row_count, dtype=jnp.int32)[None, :]
    slot = jnp.arange(slots, dtype=jnp.int32)[:, None]
    row_mask = jnp.where(is_text, mask.reshape(1, row_count), 1.0)
    slot_of = jnp.where(is_text, row // TEXT_LEN, tower_index * img_count + row // PATCHES)
    member16 = jnp.where(slot_of == slot, row_mask, 0.0).astype(jnp.bfloat16)
    share = jnp.where(is_text, 1.0 / counts, 1.0 / PATCHES)

    values = layer_input.astype(jnp.float32)
    centered = values - jnp.mean(values, axis=-1, keepdims=True)
    variance = jnp.mean(centered * centered, axis=-1, keepdims=True)
    normed = (centered * lax.rsqrt(variance + norm_eps) * gain).astype(jnp.bfloat16)
    row_mask = row_mask.reshape(row_count, 1)
    arrivals = groups_of(ring_gather(own, groups))
    plan = [(parts, rest) for parts, rest, _ in arrivals]
    share = share.astype(jnp.float32)
    cost = {"flops": int(4e9), "moved": int(16e6)}
    held_shape = jax.ShapeDtypeStruct((8, slots, shard), jnp.float32)
    slopes = []
    held = value_pool = last_pool = None
    for k, (parts, rest, (one, two)) in enumerate(arrivals):
        columns = 3 * SMALL if rest else 2 * SMALL
        slope_shape = jax.ShapeDtypeStruct((row_count, columns), jnp.bfloat16)
        shared = [share, member16]
        weights = [normed, one, two]
        if k == 0:
            slope, held, value_pool = small_call(
                functools.partial(own_kernel, parts, rest),
                (slope_shape, held_shape, jax.ShapeDtypeStruct((slots, width), jnp.float32)),
                [block_of, layer_input, *shared, row_mask, *weights],
                1,
                **cost,
            )
            slopes.append(slope)
        elif k < len(arrivals) - 1:
            slope, held = small_call(
                functools.partial(forward_kernel, parts, rest),
                (slope_shape, held_shape),
                [block_of, held, *shared, row_mask, *weights],
                1,
                **cost,
            )
            slopes.append(slope)
        else:
            last_pool = small_call(
                functools.partial(last_pool_kernel, rest),
                jax.ShapeDtypeStruct((slots, shard), jnp.float32),
                [*shared, *weights],
                0,
                **cost,
            )

    devices = 8 * groups
    pair = slots // groups
    mine = lax.all_to_all(held, "blk", 0, 0)
    opposite = []
    for place in range(8):
        for t in range(groups):
            source = RING[place] * groups + t
            opposite.append((source, RING[(place + 4) % 8] * groups + t))
    late = lax.ppermute(last_pool, ("blk", "tower"), opposite)
    partial = small_call(
        partial_kernel,
        jax.ShapeDtypeStruct((devices, pair, width), jnp.bfloat16),
        [flags, block_of, share, value_pool, mine, late, w_second],
        2,
        (
            pltpu.VMEM((8, slots, shard), jnp.float32),
            pltpu.VMEM((8 * slots, width), jnp.float32),
        ),
    )
    back = lax.all_to_all(partial, ("blk", "tower"), 0, 0)
    _, rest, (one, two) = arrivals[-1]
    slopes.append(
        small_call(
            functools.partial(late_slope_kernel, rest),
            jax.ShapeDtypeStruct((row_count, 3 * SMALL), jnp.bfloat16),
            [row_mask, normed, one, two, partial],
            0,
            flops=int(1e9),
            moved=int(4e6),
            outside=1,
        )
    )

    start = jnp.minimum(tower_index, groups - 2) * img_count
    own_positive = lax.dynamic_slice_in_dim(positives, start, img_count, 0)
    own_counts = lax.dynamic_slice_in_dim(counts[:, 0], tower_index * pair, pair, 0)
    none = jnp.zeros((pair,), jnp.int32)
    notes = jnp.stack(
        [
            jnp.zeros((2 * pair,), jnp.float32),
            jnp.zeros((2 * pair,), jnp.float32),
            jnp.concatenate([own_positive // 64, none]).astype(jnp.float32),
            jnp.concatenate([own_positive % 64, none]).astype(jnp.float32),
            jnp.concatenate([jnp.full((pair,), PATCHES, jnp.float32), own_counts]),
        ],
        axis=1,
    )
    notes = jnp.pad(notes, ((0, 0), (0, 128 - notes.shape[1])))
    copies = small_call(
        functools.partial(embed_kernel, groups),
        jax.ShapeDtypeStruct((devices, 2 * pair, width + 128), jnp.bfloat16),
        [notes, back, slopes[-1]],
        0,
        outside=1,
    )
    packed = lax.all_to_all(copies, ("blk", "tower"), 0, 0)
    packed = packed.reshape(devices * 2 * pair, width + 128)
    grad_cols, own_row = small_call(
        functools.partial(loss_kernel, groups),
        (
            jax.ShapeDtypeStruct((8, slots, shard), jnp.float32),
            jax.ShapeDtypeStruct((slots, width), jnp.float32),
        ),
        [flags, jnp.concatenate([logit_scale, logit_bias]), packed, w_second],
        2,
        (pltpu.VMEM((devices * pair, width), jnp.float32),),
    )
    grad_hidden = lax.all_to_all(grad_cols, "blk", 0, 0)
    return backward_call(
        flags,
        block_of,
        grad_hidden,
        own_row,
        row_mask,
        layer_input,
        gain,
        slopes,
        arrivals,
    )


def general_body(layer_input, caption_ids, positives, ln_gain, w_first, w_second, logit_scale, logit_bias):
    groups = lax.axis_size("tower")
    blocks = lax.axis_size("blk")
    tower_index = lax.axis_index("tower")
    block_index = lax.axis_index("blk")
    is_text = tower_index == groups - 1
    row_count, width = layer_input.shape
    slots = caption_ids.shape[0]
    img_count = positives.shape[0] // (groups - 1)
    shard = w_first.shape[2]
    gain = jnp.where(is_text, ln_gain[1], ln_gain[0])
    first = jnp.where(is_text, w_first[1].T, w_first[0].T)
    second = jnp.where(is_text, w_second[1], w_second[0])

    mask = (caption_ids != 0).astype(jnp.float32)
    counts = jnp.sum(mask, axis=1, keepdims=True)
    row = jnp.arange(row_count, dtype=jnp.int32)[None, :]
    slot = jnp.arange(slots, dtype=jnp.int32)[:, None]
    row_mask = jnp.where(is_text, mask.reshape(1, row_count), 1.0)
    member = jnp.where(jnp.where(is_text, row // TEXT_LEN, row // PATCHES) == slot, row_mask, 0.0)
    share = jnp.where(is_text, 1.0 / counts, 1.0 / PATCHES)
    member16 = member.astype(jnp.bfloat16)

    values = layer_input.astype(jnp.float32)
    centered = values - jnp.mean(values, axis=-1, keepdims=True)
    variance = jnp.mean(centered * centered, axis=-1, keepdims=True)
    inv_std = lax.rsqrt(variance + norm_eps)
    standard = centered * inv_std
    normed = (standard * gain).astype(jnp.bfloat16)
    full = lax.all_gather(first, "blk", axis=0, tiled=True)
    value, slope = gelu_pair(contract_last(normed, full))
    hidden_pool = jnp.dot(member16, value.astype(jnp.bfloat16), preferred_element_type=jnp.float32)
    hidden_pool = hidden_pool * share
    value_pool = jnp.dot(member16, layer_input, preferred_element_type=jnp.float32) * share

    sent = hidden_pool.reshape(slots, blocks, shard).transpose(1, 0, 2)
    mine = lax.all_to_all(sent, "blk", 0, 0).reshape(blocks * slots, shard)
    high, low = two_parts(mine)
    partial = jnp.dot(high, second, preferred_element_type=jnp.float32) + jnp.dot(
        low, second, preferred_element_type=jnp.float32
    )
    back = lax.all_to_all(partial.reshape(blocks, slots, width), "blk", 0, 0)
    pooled = value_pool + jnp.sum(back, axis=0)

    norm = jnp.sqrt(jnp.sum(pooled * pooled, axis=-1, keepdims=True) + norm_eps)
    emb = (pooled / norm).astype(jnp.bfloat16)
    norm_high, norm_low = two_parts(norm)
    start = jnp.minimum(tower_index, groups - 2) * img_count
    own_positive = lax.dynamic_slice_in_dim(positives, start, img_count, 0)
    own_positive = jnp.pad(own_positive, (0, slots - img_count))[:, None]
    extra = jnp.concatenate(
        [
            norm_high,
            norm_low,
            (own_positive // 64).astype(jnp.bfloat16),
            (own_positive % 64).astype(jnp.bfloat16),
            jnp.where(is_text, counts, PATCHES).astype(jnp.bfloat16),
        ],
        axis=1,
    )
    extra = jnp.pad(extra, ((0, 0), (0, 128 - extra.shape[1])))
    packed = jnp.concatenate([emb, extra], axis=1)
    packed = lax.all_to_all(
        jnp.broadcast_to(packed[None], (groups * blocks, *packed.shape)), ("tower", "blk"), 0, 0
    ).reshape(groups * blocks * slots, packed.shape[1])
    every = packed[:, :width]
    notes = packed[:, width : width + 5].astype(jnp.float32)
    every_norm = notes[:, :1] + notes[:, 1:2]
    every_positive = (notes[:, 2:3] * 64.0 + notes[:, 3:4]).astype(jnp.int32)

    scale = logit_scale[0]
    bias = logit_bias[0]
    images = (groups - 1) * blocks * slots
    column = blocks * slots
    text_emb = every[images:]
    logits = scale * contract_last(every[:images], text_emb) + bias
    caption_index = jnp.arange(column, dtype=jnp.int32)[None, :]
    onehot = (every_positive[:images] == caption_index).astype(jnp.float32)
    real = (jnp.arange(images, dtype=jnp.int32) % slots < img_count)[:, None]
    coef = jnp.where(real, loss_scale * (jax.nn.sigmoid(logits) - onehot), 0.0).astype(jnp.bfloat16)
    own = lax.dynamic_slice_in_dim(every, tower_index * column, column, 0)
    own_norm = lax.dynamic_slice_in_dim(every_norm, tower_index * column, column, 0)
    own_coef = lax.dynamic_slice_in_dim(coef, jnp.minimum(tower_index, groups - 2) * column, column, 0)
    grad_image = jnp.dot(own_coef, text_emb, preferred_element_type=jnp.float32)
    grad_text = lax.dot_general(
        coef, every[:images], (((0,), (0,)), ((), ())), preferred_element_type=jnp.float32
    )
    grad_emb = scale * jnp.where(is_text, grad_text, grad_image)
    unit = own.astype(jnp.float32)
    grad_pooled = (grad_emb - unit * jnp.sum(unit * grad_emb, axis=-1, keepdims=True)) / own_norm
    own_rows = lax.dynamic_slice_in_dim(notes[:, 4:5], tower_index * column, column, 0)
    grad_row = grad_pooled / own_rows
    grad_cols = contract_last(grad_row.astype(jnp.bfloat16), second)
    grad_hidden = lax.all_to_all(grad_cols.reshape(blocks, slots, shard), "blk", 0, 0)
    own_row = lax.dynamic_slice_in_dim(grad_row, block_index * slots, slots, 0)
    def spread(rows):
        cols = rows.shape[1]
        image = jnp.broadcast_to(
            rows[:img_count, None, :], (img_count, PATCHES, cols)
        ).reshape(row_count, cols)
        text = (rows[:, None, :] * mask[:, :, None]).reshape(row_count, cols)
        return jnp.where(is_text, text, image)

    grad_hidden = grad_hidden.transpose(1, 0, 2).reshape(slots, blocks * shard)
    grad_out = spread(own_row)
    grad_pre = (spread(grad_hidden) * slope).astype(jnp.bfloat16)
    grad_normed = jnp.dot(grad_pre, full, preferred_element_type=jnp.float32)
    grad_std = grad_normed * gain
    first_mean = jnp.mean(grad_std, axis=-1, keepdims=True)
    second_mean = jnp.mean(grad_std * standard, axis=-1, keepdims=True)
    return grad_out + inv_std * (grad_std - first_mean - standard * second_mean)


def body(layer_input, *others):
    w_first = others[3]
    ring = (
        lax.axis_size("blk") == 8
        and lax.axis_size("tower") == 4
        and w_first.shape[2] == 272
        and others[0].shape[0] == 8
        and others[1].shape[0] == 6
    )
    return (ring_body if ring else general_body)(layer_input, *others)


def solution(mesh):
    placed = (
        P(("blk", "tower"), None),
        P("blk", None),
        P("blk"),
        P(),
        P(None, None, "blk"),
        P(None, "blk", None),
        P(),
        P(),
    )
    return jax.shard_map(
        body, mesh=mesh, in_specs=placed, out_specs=P(("blk", "tower"), None), check_vma=False
    )
```

```python
import functools

import jax
import jax.numpy as jnp
from jax import lax
from jax.experimental import pallas as pl
from jax.experimental.pallas import tpu as pltpu
from jax.sharding import PartitionSpec as P

PATCHES = 256
TEXT_LEN = 64

norm_eps = 1e-06
loss_scale = 128.0
gelu_coeff = 0.7978845608028654


def gelu_pair(pre):
    inner = gelu_coeff * (pre + 0.044715 * pre * pre * pre)
    tanh_part = jnp.tanh(inner)
    value = 0.5 * pre * (1.0 + tanh_part)
    slope = 0.5 * (1.0 + tanh_part) + 0.5 * pre * (1.0 - tanh_part * tanh_part) * gelu_coeff * (
        1.0 + 3.0 * 0.044715 * pre * pre
    )
    return (value, slope)


def contract_last(left, right):
    return lax.dot_general(
        left, right, (((1,), (1,)), ((), ())), preferred_element_type=jnp.float32
    )


def two_parts(value):
    high = value.astype(jnp.bfloat16)
    low = (value - high.astype(jnp.float32)).astype(jnp.bfloat16)
    return high, low


def ring_place(block):
    return block // 2 if block % 2 == 0 else 7 - block // 2


RING = sorted(range(8), key=ring_place)


def ring_gather(own, groups):
    def move(value, step):
        found = []
        for place in range(8):
            for t in range(groups):
                source = RING[place] * groups + t
                found.append((source, RING[(place + step) % 8] * groups + t))
        return lax.ppermute(value, ("blk", "tower"), found)

    pieces = [[None, None] for _ in range(8)]
    pieces[0] = own
    for k in range(1, 5):
        for step in (1, -1):
            for chunk in (0, 1):
                if k == 4 and chunk != (0 if step == 1 else 1):
                    continue
                held = pieces[(-step * (k - 1)) % 8][chunk]
                pieces[(-step * k) % 8][chunk] = move(held, step)
    return pieces


SMALL = 128
REST = 16


def groups_of(pieces):
    found = [([(0, 0), (0, 1)], [0])]
    for k in (1, 2, 3):
        found.append(([(8 - k, 0), (k, 0)], []))
        found.append(([(8 - k, 1), (k, 1)], [8 - k, k]))
    found.append(([(4, 0), (4, 1)], [4]))
    return [(parts, rest, [pieces[p][c] for p, c in parts]) for parts, rest in found]


def project(rest, normed, one, two):
    weights = [one[:SMALL], two[:SMALL]]
    if rest:
        weights += [ref[SMALL:] for ref in (one, two) if ref.shape[0] > SMALL]
    pre = contract_last(normed[...], jnp.concatenate(weights, axis=0))
    square = pre * pre
    tanh_part = jnp.tanh(pre * (gelu_coeff + (gelu_coeff * 0.044715) * square))
    return pre, square, tanh_part, 0.5 + 0.5 * tanh_part


def slope_of(pre, square, tanh_part, gate, mask):
    bend = (0.5 * gelu_coeff) + (0.5 * gelu_coeff * 3.0 * 0.044715) * square
    slope = gate + pre * (1.0 - tanh_part * tanh_part) * bend
    return (slope * mask[...]).astype(jnp.bfloat16)


def pool_of(member, pre, gate):
    hidden = (pre * gate).astype(jnp.bfloat16)
    return jnp.dot(member[...], hidden, preferred_element_type=jnp.float32)


def put_pool(held, block_of, parts, rest, pool):
    for k, (p, c) in enumerate(parts):
        held[block_of[p], :, c * SMALL : (c + 1) * SMALL] = pool[:, k * SMALL : (k + 1) * SMALL]
    for k, p in enumerate(rest):
        start = 2 * SMALL + k * REST
        held[block_of[p], :, 2 * SMALL :] = pool[:, start : start + REST]


def own_kernel(
    parts, rest, block_of, layer_input, share, member, mask, normed, one, two, slope_ref, held, value
):
    pre, square, tanh_part, gate = project(rest, normed, one, two)
    slope = slope_of(pre, square, tanh_part, gate, mask)
    slope_ref[:, : slope.shape[1]] = slope
    held[...] = jnp.zeros_like(held)
    put_pool(held, block_of, parts, rest, pool_of(member, pre, gate) * share[...])
    value[...] = jnp.dot(member[...], layer_input[...], preferred_element_type=jnp.float32)


def forward_kernel(
    parts, rest, block_of, before, share, member, mask, normed, one, two, slope_ref, held
):
    pre, square, tanh_part, gate = project(rest, normed, one, two)
    slope = slope_of(pre, square, tanh_part, gate, mask)
    slope_ref[:, : slope.shape[1]] = slope
    held[...] = before[...]
    put_pool(held, block_of, parts, rest, pool_of(member, pre, gate) * share[...])


def last_pool_kernel(rest, share, member, normed, one, two, pool_ref):
    pre, _, _, gate = project(rest, normed, one, two)
    pool_ref[...] = pool_of(member, pre, gate) * share[...]


def late_slope_kernel(rest, mask, normed, one, two, after, slope_ref):
    slope = slope_of(*project(rest, normed, one, two), mask)
    slope_ref[:, : slope.shape[1]] = slope


def backward_kernel(
    plan, flags, block_of, grad_hidden, own_row, gain, mask, layer_input, *refs
):
    count = len(plan)
    slopes = refs[:count]
    weight_refs = refs[count : 3 * count]
    out = refs[3 * count]
    is_text = flags[0] == 1
    step = pl.program_id(0)
    tile = layer_input.shape[0]
    bands = [pl.ds(k * TEXT_LEN, TEXT_LEN) for k in range(tile // TEXT_LEN)]
    slots = [
        jnp.where(
            is_text,
            step * len(bands) + k,
            flags[1] + (step * len(bands) + k) * TEXT_LEN // PATCHES,
        )
        for k in range(len(bands))
    ]
    def pick(lines, slot):
        row = lax.broadcasted_iota(jnp.int32, lines.shape, 0)
        return jnp.sum(jnp.where(row == slot, lines, 0.0), axis=0, keepdims=True)

    def scaled(slope_ref, start, lines):
        found = []
        for band, slot in zip(bands, slots):
            slope = slope_ref[band, start : start + lines.shape[1]].astype(jnp.float32)
            found.append((pick(lines, slot) * slope).astype(jnp.bfloat16))
        return jnp.concatenate(found, axis=0)

    def multiply(left, parts):
        right = jnp.concatenate(parts, axis=0)
        return jnp.dot(left, right, preferred_element_type=jnp.float32)

    def main_part(g):
        parts, _ = plan[g]
        lines = [grad_hidden[block_of[p], :, c * SMALL : (c + 1) * SMALL] for p, c in parts]
        return scaled(slopes[g], 0, jnp.concatenate(lines, axis=1))

    def rest_part(g):
        _, rest = plan[g]
        lines = [grad_hidden[block_of[p], :, 2 * SMALL :] for p in rest]
        return scaled(slopes[g], 2 * SMALL, jnp.concatenate(lines, axis=1))

    rests = [rest_part(g) for g in range(count) if plan[g][1]]
    total = None
    for g in range(0, count, 2):
        left = jnp.concatenate([main_part(g), main_part(g + 1)], axis=1)
        product = multiply(left, [ref[:SMALL] for ref in weight_refs[2 * g : 2 * g + 4]])
        total = product if total is None else total + product
    tails = [ref[SMALL:] for ref in weight_refs if ref.shape[0] > SMALL]
    total = total + multiply(jnp.concatenate(rests, axis=1), tails)

    values = layer_input[...].astype(jnp.float32)
    centered = values - jnp.mean(values, axis=-1, keepdims=True)
    variance = jnp.mean(centered * centered, axis=-1, keepdims=True)
    inv_std = lax.rsqrt(variance + norm_eps)
    standard = centered * inv_std
    grad_std = total * gain[...]
    first_mean = jnp.mean(grad_std, axis=-1, keepdims=True)
    second_mean = jnp.mean(grad_std * standard, axis=-1, keepdims=True)
    result = inv_std * (grad_std - first_mean - standard * second_mean)
    for k, (band, slot) in enumerate(zip(bands, slots)):
        grad_out = pick(own_row[...], slot) * mask[band, :]
        out[band, :] = grad_out + result[k * TEXT_LEN : (k + 1) * TEXT_LEN]


def backward_call(flags, block_of, grad_hidden, own_row, mask, layer_input, gain, slopes, groups):
    row_count, width = layer_input.shape
    tile = 4 * TEXT_LEN
    whole = pl.BlockSpec(memory_space=pltpu.VMEM)
    scalar = pl.BlockSpec(memory_space=pltpu.SMEM)

    def by_rows(cols):
        return pl.BlockSpec((tile, cols), lambda i: (i, 0))

    plan = [(parts, rest) for parts, rest, _ in groups]
    weights = [w for _, _, pair in groups for w in pair]
    count = len(plan)
    units = sum(w.shape[0] for w in weights)
    return pl.pallas_call(
        functools.partial(backward_kernel, plan),
        grid=(row_count // tile,),
        in_specs=[scalar] * 2
        + [whole] * 3
        + [by_rows(1), by_rows(width)]
        + [by_rows(slope.shape[1]) for slope in slopes]
        + [whole] * (2 * count),
        out_specs=by_rows(width),
        out_shape=jax.ShapeDtypeStruct((row_count, width), jnp.float32),
        compiler_params=pltpu.CompilerParams(vmem_limit_bytes=60 * 1024 * 1024),
        cost_estimate=pl.CostEstimate(
            flops=2 * row_count * width * units, bytes_accessed=12_000_000, transcendentals=0
        ),
    )(
        flags,
        block_of,
        grad_hidden,
        own_row,
        gain.reshape(1, width),
        mask,
        layer_input,
        *slopes,
        *weights,
    )


def partial_kernel(flags, block_of, share, value_pool, mine, late, w_second, out, pools, rows):
    slots, shard = late.shape
    pools[...] = mine[...]
    pools[block_of[4]] = late[...]
    high, low = two_parts(pools[...].reshape(8 * slots, shard))
    second = w_second[flags[0]]
    both = jnp.dot(
        jnp.concatenate([high, low], axis=0), second, preferred_element_type=jnp.float32
    )
    rows[...] = both[: 8 * slots] + both[8 * slots :]
    own = pl.ds(pl.multiple_of(flags[2] * slots, slots), slots)
    rows[own, :] += value_pool[...] * share[...]
    pair = out.shape[1]
    for k in range(out.shape[0]):
        out[k] = rows[k * pair : (k + 1) * pair, :].astype(out.dtype)


def embed_kernel(groups, notes, back, *refs):
    out = refs[-1]

    def total(places):
        found = back[places[0]].astype(jnp.float32)
        for place in places[1:]:
            found = found + back[place].astype(jnp.float32)
        return found

    devices = range(back.shape[0])
    image = total([d for d in devices if d % groups < groups - 1])
    text = total([d for d in devices if d % groups == groups - 1])
    pooled = jnp.concatenate([image, text], axis=0)
    norm = jnp.sqrt(jnp.sum(pooled * pooled, axis=-1, keepdims=True) + norm_eps)
    emb = (pooled / norm).astype(jnp.bfloat16)
    high = norm.astype(jnp.bfloat16).astype(jnp.float32)
    lane = lax.broadcasted_iota(jnp.int32, notes.shape, 1)
    marks = jnp.where(lane == 0, high, jnp.where(lane == 1, norm - high, notes[...]))
    row = jnp.concatenate([emb, marks.astype(jnp.bfloat16)], axis=1)
    out[...] = jnp.broadcast_to(row[None], out.shape)


def loss_kernel(groups, flags, scalars, packed, w_second, grad_cols, own_row, rows_ref):
    is_text = flags[0] == 1
    scale, bias = scalars[0], scalars[1]
    count, total_width = packed.shape
    width = own_row.shape[1]
    half = count // 2
    row = lax.broadcasted_iota(jnp.int32, (half, count), 0)
    column = lax.broadcasted_iota(jnp.int32, (half, count), 1)
    place = 4 * (row // 2) + row % 2
    everything = packed[...]

    def chosen(offset):
        which = (column == place + offset).astype(jnp.bfloat16)
        return jnp.dot(which, everything, preferred_element_type=jnp.float32)

    image, text = chosen(0), chosen(2)
    image16 = image[:, :width].astype(jnp.bfloat16)
    text16 = text[:, :width].astype(jnp.bfloat16)
    logits = scale * contract_last(image16, text16) + bias
    positive = image[:, width + 2 : width + 3] * 64.0 + image[:, width + 3 : width + 4]
    row = lax.broadcasted_iota(jnp.int32, (half, half), 0)
    column = lax.broadcasted_iota(jnp.int32, (half, half), 1)
    onehot = (column.astype(jnp.float32) == positive).astype(jnp.float32)
    sigmoid = 1.0 / (1.0 + jnp.exp(-logits))
    real = row % (2 * groups) < 2 * (groups - 1)
    coef = jnp.where(real, loss_scale * (sigmoid - onehot), 0.0)
    left = jnp.where(is_text, coef.T, coef).astype(jnp.bfloat16)
    right = jnp.where(is_text, image16, text16)
    grad_emb = scale * jnp.dot(left, right, preferred_element_type=jnp.float32)
    own = jnp.where(is_text, text, image)
    unit = own[:, :width]
    norm = own[:, width : width + 1] + own[:, width + 1 : width + 2]
    rows = own[:, width + 4 : width + 5]
    grad_pooled = grad_emb - unit * jnp.sum(unit * grad_emb, axis=-1, keepdims=True)
    grad_row = grad_pooled / (norm * rows)
    rows_ref[...] = grad_row
    own_row[...] = rows_ref[pl.ds(pl.multiple_of(flags[2] * 8, 8), 8), :]
    second = w_second[flags[0]]
    columns = contract_last(grad_row.astype(jnp.bfloat16), second)
    for block in range(grad_cols.shape[0]):
        grad_cols[block] = columns[block * 8 : (block + 1) * 8]


def small_call(kernel, outs, operands, scalars, scratch=(), flops=0, moved=0, outside=0):
    single = not isinstance(outs, tuple)
    whole = pl.BlockSpec(memory_space=pltpu.VMEM)
    scalar = pl.BlockSpec(memory_space=pltpu.SMEM)
    return pl.pallas_call(
        kernel,
        in_specs=[scalar] * scalars
        + [whole] * (len(operands) - scalars - outside)
        + [pl.BlockSpec(memory_space=pl.ANY)] * outside,
        out_specs=whole if single else tuple(whole for _ in outs),
        out_shape=outs,
        scratch_shapes=scratch,
        compiler_params=pltpu.CompilerParams(vmem_limit_bytes=16 * 1024 * 1024),
        cost_estimate=pl.CostEstimate(flops=flops, bytes_accessed=moved, transcendentals=0),
    )(*operands)


def ring_body(
    layer_input, caption_ids, positives, ln_gain, w_first, w_second, logit_scale, logit_bias
):
    groups = lax.axis_size("tower")
    tower_index = lax.axis_index("tower")
    block_index = lax.axis_index("blk")
    is_text = tower_index == groups - 1
    row_count, width = layer_input.shape
    slots = caption_ids.shape[0]
    img_count = positives.shape[0] // (groups - 1)
    shard = w_first.shape[2]
    gain = jnp.where(is_text, ln_gain[1], ln_gain[0])
    own = [
        jnp.where(is_text, w_first[1, :, cut].T, w_first[0, :, cut].T)
        for cut in (slice(0, SMALL), slice(SMALL, shard))
    ]
    flags = jnp.stack([is_text.astype(jnp.int32), tower_index * img_count, block_index])
    flags = flags.astype(jnp.int32)
    place = jnp.where(block_index % 2 == 0, block_index // 2, 7 - block_index // 2)
    around = (place + jnp.arange(8, dtype=jnp.int32)) % 8
    block_of = jnp.where(around < 4, 2 * around, 2 * (7 - around) + 1).astype(jnp.int32)

    mask = (caption_ids != 0).astype(jnp.float32)
    counts = jnp.sum(mask, axis=1, keepdims=True)
    row = jnp.arange(row_count, dtype=jnp.int32)[None, :]
    slot = jnp.arange(slots, dtype=jnp.int32)[:, None]
    row_mask = jnp.where(is_text, mask.reshape(1, row_count), 1.0)
    slot_of = jnp.where(is_text, row // TEXT_LEN, tower_index * img_count + row // PATCHES)
    member16 = jnp.where(slot_of == slot, row_mask, 0.0).astype(jnp.bfloat16)
    share = jnp.where(is_text, 1.0 / counts, 1.0 / PATCHES)

    values = layer_input.astype(jnp.float32)
    centered = values - jnp.mean(values, axis=-1, keepdims=True)
    variance = jnp.mean(centered * centered, axis=-1, keepdims=True)
    normed = (centered * lax.rsqrt(variance + norm_eps) * gain).astype(jnp.bfloat16)
    row_mask = row_mask.reshape(row_count, 1)
    arrivals = groups_of(ring_gather(own, groups))
    plan = [(parts, rest) for parts, rest, _ in arrivals]
    share = share.astype(jnp.float32)
    cost = {"flops": int(4e9), "moved": int(16e6)}
    held_shape = jax.ShapeDtypeStruct((8, slots, shard), jnp.float32)
    slopes = []
    held = value_pool = last_pool = None
    for k, (parts, rest, (one, two)) in enumerate(arrivals):
        columns = 3 * SMALL if rest else 2 * SMALL
        slope_shape = jax.ShapeDtypeStruct((row_count, columns), jnp.bfloat16)
        shared = [share, member16]
        weights = [normed, one, two]
        if k == 0:
            slope, held, value_pool = small_call(
                functools.partial(own_kernel, parts, rest),
                (slope_shape, held_shape, jax.ShapeDtypeStruct((slots, width), jnp.float32)),
                [block_of, layer_input, *shared, row_mask, *weights],
                1,
                **cost,
            )
            slopes.append(slope)
        elif k < len(arrivals) - 1:
            slope, held = small_call(
                functools.partial(forward_kernel, parts, rest),
                (slope_shape, held_shape),
                [block_of, held, *shared, row_mask, *weights],
                1,
                **cost,
            )
            slopes.append(slope)
        else:
            last_pool = small_call(
                functools.partial(last_pool_kernel, rest),
                jax.ShapeDtypeStruct((slots, shard), jnp.float32),
                [*shared, *weights],
                0,
                **cost,
            )

    devices = 8 * groups
    pair = slots // groups
    mine = lax.all_to_all(held, "blk", 0, 0)
    opposite = []
    for place in range(8):
        for t in range(groups):
            source = RING[place] * groups + t
            opposite.append((source, RING[(place + 4) % 8] * groups + t))
    late = lax.ppermute(last_pool, ("blk", "tower"), opposite)
    partial = small_call(
        partial_kernel,
        jax.ShapeDtypeStruct((devices, pair, width), jnp.bfloat16),
        [flags, block_of, share, value_pool, mine, late, w_second],
        2,
        (
            pltpu.VMEM((8, slots, shard), jnp.float32),
            pltpu.VMEM((8 * slots, width), jnp.float32),
        ),
    )
    back = lax.all_to_all(partial, ("blk", "tower"), 0, 0)
    _, rest, (one, two) = arrivals[-1]
    slopes.append(
        small_call(
            functools.partial(late_slope_kernel, rest),
            jax.ShapeDtypeStruct((row_count, 3 * SMALL), jnp.bfloat16),
            [row_mask, normed, one, two, partial],
            0,
            flops=int(1e9),
            moved=int(4e6),
            outside=1,
        )
    )

    start = jnp.minimum(tower_index, groups - 2) * img_count
    own_positive = lax.dynamic_slice_in_dim(positives, start, img_count, 0)
    own_counts = lax.dynamic_slice_in_dim(counts[:, 0], tower_index * pair, pair, 0)
    none = jnp.zeros((pair,), jnp.int32)
    notes = jnp.stack(
        [
            jnp.zeros((2 * pair,), jnp.float32),
            jnp.zeros((2 * pair,), jnp.float32),
            jnp.concatenate([own_positive // 64, none]).astype(jnp.float32),
            jnp.concatenate([own_positive % 64, none]).astype(jnp.float32),
            jnp.concatenate([jnp.full((pair,), PATCHES, jnp.float32), own_counts]),
        ],
        axis=1,
    )
    notes = jnp.pad(notes, ((0, 0), (0, 128 - notes.shape[1])))
    copies = small_call(
        functools.partial(embed_kernel, groups),
        jax.ShapeDtypeStruct((devices, 2 * pair, width + 128), jnp.bfloat16),
        [notes, back, slopes[-1]],
        0,
        outside=1,
    )
    packed = lax.all_to_all(copies, ("blk", "tower"), 0, 0)
    packed = packed.reshape(devices * 2 * pair, width + 128)
    grad_cols, own_row = small_call(
        functools.partial(loss_kernel, groups),
        (
            jax.ShapeDtypeStruct((8, slots, shard), jnp.float32),
            jax.ShapeDtypeStruct((slots, width), jnp.float32),
        ),
        [flags, jnp.concatenate([logit_scale, logit_bias]), packed, w_second],
        2,
        (pltpu.VMEM((devices * pair, width), jnp.float32),),
    )
    grad_hidden = lax.all_to_all(grad_cols, "blk", 0, 0)
    return backward_call(
        flags,
        block_of,
        grad_hidden,
        own_row,
        row_mask,
        layer_input,
        gain,
        slopes,
        arrivals,
    )


def general_body(layer_input, caption_ids, positives, ln_gain, w_first, w_second, logit_scale, logit_bias):
    groups = lax.axis_size("tower")
    blocks = lax.axis_size("blk")
    tower_index = lax.axis_index("tower")
    block_index = lax.axis_index("blk")
    is_text = tower_index == groups - 1
    row_count, width = layer_input.shape
    slots = caption_ids.shape[0]
    img_count = positives.shape[0] // (groups - 1)
    shard = w_first.shape[2]
    gain = jnp.where(is_text, ln_gain[1], ln_gain[0])
    first = jnp.where(is_text, w_first[1].T, w_first[0].T)
    second = jnp.where(is_text, w_second[1], w_second[0])

    mask = (caption_ids != 0).astype(jnp.float32)
    counts = jnp.sum(mask, axis=1, keepdims=True)
    row = jnp.arange(row_count, dtype=jnp.int32)[None, :]
    slot = jnp.arange(slots, dtype=jnp.int32)[:, None]
    row_mask = jnp.where(is_text, mask.reshape(1, row_count), 1.0)
    member = jnp.where(jnp.where(is_text, row // TEXT_LEN, row // PATCHES) == slot, row_mask, 0.0)
    share = jnp.where(is_text, 1.0 / counts, 1.0 / PATCHES)
    member16 = member.astype(jnp.bfloat16)

    values = layer_input.astype(jnp.float32)
    centered = values - jnp.mean(values, axis=-1, keepdims=True)
    variance = jnp.mean(centered * centered, axis=-1, keepdims=True)
    inv_std = lax.rsqrt(variance + norm_eps)
    standard = centered * inv_std
    normed = (standard * gain).astype(jnp.bfloat16)
    full = lax.all_gather(first, "blk", axis=0, tiled=True)
    value, slope = gelu_pair(contract_last(normed, full))
    hidden_pool = jnp.dot(member16, value.astype(jnp.bfloat16), preferred_element_type=jnp.float32)
    hidden_pool = hidden_pool * share
    value_pool = jnp.dot(member16, layer_input, preferred_element_type=jnp.float32) * share

    sent = hidden_pool.reshape(slots, blocks, shard).transpose(1, 0, 2)
    mine = lax.all_to_all(sent, "blk", 0, 0).reshape(blocks * slots, shard)
    high, low = two_parts(mine)
    partial = jnp.dot(high, second, preferred_element_type=jnp.float32) + jnp.dot(
        low, second, preferred_element_type=jnp.float32
    )
    back = lax.all_to_all(partial.reshape(blocks, slots, width), "blk", 0, 0)
    pooled = value_pool + jnp.sum(back, axis=0)

    norm = jnp.sqrt(jnp.sum(pooled * pooled, axis=-1, keepdims=True) + norm_eps)
    emb = (pooled / norm).astype(jnp.bfloat16)
    norm_high, norm_low = two_parts(norm)
    start = jnp.minimum(tower_index, groups - 2) * img_count
    own_positive = lax.dynamic_slice_in_dim(positives, start, img_count, 0)
    own_positive = jnp.pad(own_positive, (0, slots - img_count))[:, None]
    extra = jnp.concatenate(
        [
            norm_high,
            norm_low,
            (own_positive // 64).astype(jnp.bfloat16),
            (own_positive % 64).astype(jnp.bfloat16),
            jnp.where(is_text, counts, PATCHES).astype(jnp.bfloat16),
        ],
        axis=1,
    )
    extra = jnp.pad(extra, ((0, 0), (0, 128 - extra.shape[1])))
    packed = jnp.concatenate([emb, extra], axis=1)
    packed = lax.all_to_all(
        jnp.broadcast_to(packed[None], (groups * blocks, *packed.shape)), ("tower", "blk"), 0, 0
    ).reshape(groups * blocks * slots, packed.shape[1])
    every = packed[:, :width]
    notes = packed[:, width : width + 5].astype(jnp.float32)
    every_norm = notes[:, :1] + notes[:, 1:2]
    every_positive = (notes[:, 2:3] * 64.0 + notes[:, 3:4]).astype(jnp.int32)

    scale = logit_scale[0]
    bias = logit_bias[0]
    images = (groups - 1) * blocks * slots
    column = blocks * slots
    text_emb = every[images:]
    logits = scale * contract_last(every[:images], text_emb) + bias
    caption_index = jnp.arange(column, dtype=jnp.int32)[None, :]
    onehot = (every_positive[:images] == caption_index).astype(jnp.float32)
    real = (jnp.arange(images, dtype=jnp.int32) % slots < img_count)[:, None]
    coef = jnp.where(real, loss_scale * (jax.nn.sigmoid(logits) - onehot), 0.0).astype(jnp.bfloat16)
    own = lax.dynamic_slice_in_dim(every, tower_index * column, column, 0)
    own_norm = lax.dynamic_slice_in_dim(every_norm, tower_index * column, column, 0)
    own_coef = lax.dynamic_slice_in_dim(coef, jnp.minimum(tower_index, groups - 2) * column, column, 0)
    grad_image = jnp.dot(own_coef, text_emb, preferred_element_type=jnp.float32)
    grad_text = lax.dot_general(
        coef, every[:images], (((0,), (0,)), ((), ())), preferred_element_type=jnp.float32
    )
    grad_emb = scale * jnp.where(is_text, grad_text, grad_image)
    unit = own.astype(jnp.float32)
    grad_pooled = (grad_emb - unit * jnp.sum(unit * grad_emb, axis=-1, keepdims=True)) / own_norm
    own_rows = lax.dynamic_slice_in_dim(notes[:, 4:5], tower_index * column, column, 0)
    grad_row = grad_pooled / own_rows
    grad_cols = contract_last(grad_row.astype(jnp.bfloat16), second)
    grad_hidden = lax.all_to_all(grad_cols.reshape(blocks, slots, shard), "blk", 0, 0)
    own_row = lax.dynamic_slice_in_dim(grad_row, block_index * slots, slots, 0)
    def spread(rows):
        cols = rows.shape[1]
        image = jnp.broadcast_to(
            rows[:img_count, None, :], (img_count, PATCHES, cols)
        ).reshape(row_count, cols)
        text = (rows[:, None, :] * mask[:, :, None]).reshape(row_count, cols)
        return jnp.where(is_text, text, image)

    grad_hidden = grad_hidden.transpose(1, 0, 2).reshape(slots, blocks * shard)
    grad_out = spread(own_row)
    grad_pre = (spread(grad_hidden) * slope).astype(jnp.bfloat16)
    grad_normed = jnp.dot(grad_pre, full, preferred_element_type=jnp.float32)
    grad_std = grad_normed * gain
    first_mean = jnp.mean(grad_std, axis=-1, keepdims=True)
    second_mean = jnp.mean(grad_std * standard, axis=-1, keepdims=True)
    return grad_out + inv_std * (grad_std - first_mean - standard * second_mean)


def body(layer_input, *others):
    w_first = others[3]
    ring = (
        lax.axis_size("blk") == 8
        and lax.axis_size("tower") == 4
        and w_first.shape[2] == 272
        and others[0].shape[0] == 8
        and others[1].shape[0] == 6
    )
    return (ring_body if ring else general_body)(layer_input, *others)


def solution(mesh):
    placed = (
        P(("blk", "tower"), None),
        P("blk", None),
        P("blk"),
        P(),
        P(None, None, "blk"),
        P(None, "blk", None),
        P(),
        P(),
    )
    return jax.shard_map(
        body, mesh=mesh, in_specs=placed, out_specs=P(("blk", "tower"), None), check_vma=False
    )
```

```python
import functools

import jax
import jax.numpy as jnp
from jax import lax
from jax.experimental import pallas as pl
from jax.experimental.pallas import tpu as pltpu
from jax.sharding import PartitionSpec as P

PATCHES = 256
TEXT_LEN = 64

norm_eps = 1e-06
loss_scale = 128.0
gelu_coeff = 0.7978845608028654


def gelu_pair(pre):
    inner = gelu_coeff * (pre + 0.044715 * pre * pre * pre)
    tanh_part = jnp.tanh(inner)
    value = 0.5 * pre * (1.0 + tanh_part)
    slope = 0.5 * (1.0 + tanh_part) + 0.5 * pre * (1.0 - tanh_part * tanh_part) * gelu_coeff * (
        1.0 + 3.0 * 0.044715 * pre * pre
    )
    return (value, slope)


def contract_last(left, right):
    return lax.dot_general(
        left, right, (((1,), (1,)), ((), ())), preferred_element_type=jnp.float32
    )


def two_parts(value):
    high = value.astype(jnp.bfloat16)
    low = (value - high.astype(jnp.float32)).astype(jnp.bfloat16)
    return high, low


def ring_place(block):
    return block // 2 if block % 2 == 0 else 7 - block // 2


RING = sorted(range(8), key=ring_place)


def ring_gather(own, groups):
    def move(value, step):
        found = []
        for place in range(8):
            for t in range(groups):
                source = RING[place] * groups + t
                found.append((source, RING[(place + step) % 8] * groups + t))
        return lax.ppermute(value, ("blk", "tower"), found)

    pieces = [[None, None] for _ in range(8)]
    pieces[0] = own
    for k in range(1, 5):
        for step in (1, -1):
            for chunk in (0, 1):
                if k == 4 and chunk != (0 if step == 1 else 1):
                    continue
                held = pieces[(-step * (k - 1)) % 8][chunk]
                pieces[(-step * k) % 8][chunk] = move(held, step)
    return pieces


SMALL = 128
REST = 16


def groups_of(pieces):
    found = [([(0, 0), (0, 1)], [0])]
    for k in (1, 2, 3):
        found.append(([(8 - k, 0), (k, 0)], []))
        found.append(([(8 - k, 1), (k, 1)], [8 - k, k]))
    found.append(([(4, 0), (4, 1)], [4]))
    return [(parts, rest, [pieces[p][c] for p, c in parts]) for parts, rest in found]


def project(rest, normed, one, two):
    weights = [one[:SMALL], two[:SMALL]]
    if rest:
        weights += [ref[SMALL:] for ref in (one, two) if ref.shape[0] > SMALL]
    pre = contract_last(normed[...], jnp.concatenate(weights, axis=0))
    square = pre * pre
    tanh_part = jnp.tanh(pre * (gelu_coeff + (gelu_coeff * 0.044715) * square))
    return pre, square, tanh_part, 0.5 + 0.5 * tanh_part


def slope_of(pre, square, tanh_part, gate, mask):
    bend = (0.5 * gelu_coeff) + (0.5 * gelu_coeff * 3.0 * 0.044715) * square
    slope = gate + pre * (1.0 - tanh_part * tanh_part) * bend
    return (slope * mask[...]).astype(jnp.bfloat16)


def pool_of(member, pre, gate):
    hidden = (pre * gate).astype(jnp.bfloat16)
    return jnp.dot(member[...], hidden, preferred_element_type=jnp.float32)


def put_pool(held, block_of, parts, rest, pool):
    for k, (p, c) in enumerate(parts):
        held[block_of[p], :, c * SMALL : (c + 1) * SMALL] = pool[:, k * SMALL : (k + 1) * SMALL]
    for k, p in enumerate(rest):
        start = 2 * SMALL + k * REST
        held[block_of[p], :, 2 * SMALL :] = pool[:, start : start + REST]


def own_kernel(
    parts, rest, block_of, layer_input, share, member, mask, normed, one, two, slope_ref, held, value
):
    pre, square, tanh_part, gate = project(rest, normed, one, two)
    slope = slope_of(pre, square, tanh_part, gate, mask)
    slope_ref[:, : slope.shape[1]] = slope
    held[...] = jnp.zeros_like(held)
    put_pool(held, block_of, parts, rest, pool_of(member, pre, gate) * share[...])
    value[...] = jnp.dot(member[...], layer_input[...], preferred_element_type=jnp.float32)


def forward_kernel(
    parts, rest, block_of, before, share, member, mask, normed, one, two, slope_ref, held
):
    pre, square, tanh_part, gate = project(rest, normed, one, two)
    slope = slope_of(pre, square, tanh_part, gate, mask)
    slope_ref[:, : slope.shape[1]] = slope
    held[...] = before[...]
    put_pool(held, block_of, parts, rest, pool_of(member, pre, gate) * share[...])


def edge_kernel(
    rest, share, member, mask, normed, one, two, slope_ref, low_pool, high_pool
):
    pre, square, tanh_part, gate = project(rest, normed, one, two)
    slope = slope_of(pre, square, tanh_part, gate, mask)
    slope_ref[:, : slope.shape[1]] = slope
    pool = pool_of(member, pre, gate) * share[...]
    for k, ref in enumerate((low_pool, high_pool)):
        start = 2 * SMALL + k * REST
        ref[:, :SMALL] = pool[:, k * SMALL : (k + 1) * SMALL]
        ref[:, SMALL:] = pool[:, start : start + REST]


def last_pool_kernel(rest, share, member, normed, one, two, pool_ref):
    pre, _, _, gate = project(rest, normed, one, two)
    pool_ref[...] = pool_of(member, pre, gate) * share[...]


def late_slope_kernel(rest, mask, normed, one, two, after, slope_ref):
    slope = slope_of(*project(rest, normed, one, two), mask)
    slope_ref[:, : slope.shape[1]] = slope


def backward_kernel(
    plan, flags, block_of, grad_hidden, own_row, gain, mask, layer_input, *refs
):
    count = len(plan)
    slopes = refs[:count]
    weight_refs = refs[count : 3 * count]
    out = refs[3 * count]
    is_text = flags[0] == 1
    step = pl.program_id(0)
    tile = layer_input.shape[0]
    bands = [pl.ds(k * TEXT_LEN, TEXT_LEN) for k in range(tile // TEXT_LEN)]
    slots = [
        jnp.where(
            is_text,
            step * len(bands) + k,
            flags[1] + (step * len(bands) + k) * TEXT_LEN // PATCHES,
        )
        for k in range(len(bands))
    ]
    def pick(lines, slot):
        row = lax.broadcasted_iota(jnp.int32, lines.shape, 0)
        return jnp.sum(jnp.where(row == slot, lines, 0.0), axis=0, keepdims=True)

    def scaled(slope_ref, start, lines):
        found = []
        for band, slot in zip(bands, slots):
            slope = slope_ref[band, start : start + lines.shape[1]].astype(jnp.float32)
            found.append((pick(lines, slot) * slope).astype(jnp.bfloat16))
        return jnp.concatenate(found, axis=0)

    def multiply(left, parts):
        right = jnp.concatenate(parts, axis=0)
        return jnp.dot(left, right, preferred_element_type=jnp.float32)

    def main_part(g):
        parts, _ = plan[g]
        lines = [grad_hidden[block_of[p], :, c * SMALL : (c + 1) * SMALL] for p, c in parts]
        return scaled(slopes[g], 0, jnp.concatenate(lines, axis=1))

    def rest_part(g):
        _, rest = plan[g]
        lines = [grad_hidden[block_of[p], :, 2 * SMALL :] for p in rest]
        return scaled(slopes[g], 2 * SMALL, jnp.concatenate(lines, axis=1))

    rests = [rest_part(g) for g in range(count) if plan[g][1]]
    total = None
    for g in range(0, count, 2):
        left = jnp.concatenate([main_part(g), main_part(g + 1)], axis=1)
        product = multiply(left, [ref[:SMALL] for ref in weight_refs[2 * g : 2 * g + 4]])
        total = product if total is None else total + product
    tails = [ref[SMALL:] for ref in weight_refs if ref.shape[0] > SMALL]
    total = total + multiply(jnp.concatenate(rests, axis=1), tails)

    values = layer_input[...].astype(jnp.float32)
    centered = values - jnp.mean(values, axis=-1, keepdims=True)
    variance = jnp.mean(centered * centered, axis=-1, keepdims=True)
    inv_std = lax.rsqrt(variance + norm_eps)
    standard = centered * inv_std
    grad_std = total * gain[...]
    first_mean = jnp.mean(grad_std, axis=-1, keepdims=True)
    second_mean = jnp.mean(grad_std * standard, axis=-1, keepdims=True)
    result = inv_std * (grad_std - first_mean - standard * second_mean)
    for k, (band, slot) in enumerate(zip(bands, slots)):
        grad_out = pick(own_row[...], slot) * mask[band, :]
        out[band, :] = grad_out + result[k * TEXT_LEN : (k + 1) * TEXT_LEN]


def backward_call(flags, block_of, grad_hidden, own_row, mask, layer_input, gain, slopes, groups):
    row_count, width = layer_input.shape
    tile = 2 * TEXT_LEN
    whole = pl.BlockSpec(memory_space=pltpu.VMEM)
    scalar = pl.BlockSpec(memory_space=pltpu.SMEM)

    def by_rows(cols):
        return pl.BlockSpec((tile, cols), lambda i: (i, 0))

    plan = [(parts, rest) for parts, rest, _ in groups]
    weights = [w for _, _, pair in groups for w in pair]
    count = len(plan)
    units = sum(w.shape[0] for w in weights)
    return pl.pallas_call(
        functools.partial(backward_kernel, plan),
        grid=(row_count // tile,),
        in_specs=[scalar] * 2
        + [whole] * 3
        + [by_rows(1), by_rows(width)]
        + [by_rows(slope.shape[1]) for slope in slopes]
        + [whole] * (2 * count),
        out_specs=by_rows(width),
        out_shape=jax.ShapeDtypeStruct((row_count, width), jnp.float32),
        compiler_params=pltpu.CompilerParams(vmem_limit_bytes=60 * 1024 * 1024),
        cost_estimate=pl.CostEstimate(
            flops=2 * row_count * width * units, bytes_accessed=12_000_000, transcendentals=0
        ),
    )(
        flags,
        block_of,
        grad_hidden,
        own_row,
        gain.reshape(1, width),
        mask,
        layer_input,
        *slopes,
        *weights,
    )


def partial_kernel(
    flags, block_of, share, value_pool, mine, late, from_3, from_5, w_second, out, pools, rows
):
    slots, shard = late.shape
    pools[...] = mine[...]
    pools[block_of[4]] = late[...]
    pools[block_of[3], :, SMALL:] = from_3[...]
    pools[block_of[5], :, SMALL:] = from_5[...]
    high, low = two_parts(pools[...].reshape(8 * slots, shard))
    second = w_second[flags[0]]
    both = jnp.dot(
        jnp.concatenate([high, low], axis=0), second, preferred_element_type=jnp.float32
    )
    rows[...] = both[: 8 * slots] + both[8 * slots :]
    own = pl.ds(pl.multiple_of(flags[2] * slots, slots), slots)
    rows[own, :] += value_pool[...] * share[...]
    pair = out.shape[1]
    for k in range(out.shape[0]):
        out[k] = rows[k * pair : (k + 1) * pair, :].astype(out.dtype)


def embed_kernel(groups, notes, back, *refs):
    out = refs[-1]

    def total(places):
        found = back[places[0]].astype(jnp.float32)
        for place in places[1:]:
            found = found + back[place].astype(jnp.float32)
        return found

    devices = range(back.shape[0])
    image = total([d for d in devices if d % groups < groups - 1])
    text = total([d for d in devices if d % groups == groups - 1])
    pooled = jnp.concatenate([image, text], axis=0)
    norm = jnp.sqrt(jnp.sum(pooled * pooled, axis=-1, keepdims=True) + norm_eps)
    emb = (pooled / norm).astype(jnp.bfloat16)
    high = norm.astype(jnp.bfloat16).astype(jnp.float32)
    lane = lax.broadcasted_iota(jnp.int32, notes.shape, 1)
    marks = jnp.where(lane == 0, high, jnp.where(lane == 1, norm - high, notes[...]))
    row = jnp.concatenate([emb, marks.astype(jnp.bfloat16)], axis=1)
    out[...] = jnp.broadcast_to(row[None], out.shape)


def loss_kernel(groups, flags, scalars, packed, w_second, grad_cols, own_row, rows_ref):
    is_text = flags[0] == 1
    scale, bias = scalars[0], scalars[1]
    count, total_width = packed.shape
    width = own_row.shape[1]
    half = count // 2
    row = lax.broadcasted_iota(jnp.int32, (half, count), 0)
    column = lax.broadcasted_iota(jnp.int32, (half, count), 1)
    place = 4 * (row // 2) + row % 2
    everything = packed[...]

    def chosen(offset):
        which = (column == place + offset).astype(jnp.bfloat16)
        return jnp.dot(which, everything, preferred_element_type=jnp.float32)

    image, text = chosen(0), chosen(2)
    image16 = image[:, :width].astype(jnp.bfloat16)
    text16 = text[:, :width].astype(jnp.bfloat16)
    logits = scale * contract_last(image16, text16) + bias
    positive = image[:, width + 2 : width + 3] * 64.0 + image[:, width + 3 : width + 4]
    row = lax.broadcasted_iota(jnp.int32, (half, half), 0)
    column = lax.broadcasted_iota(jnp.int32, (half, half), 1)
    onehot = (column.astype(jnp.float32) == positive).astype(jnp.float32)
    sigmoid = 1.0 / (1.0 + jnp.exp(-logits))
    real = row % (2 * groups) < 2 * (groups - 1)
    coef = jnp.where(real, loss_scale * (sigmoid - onehot), 0.0)
    left = jnp.where(is_text, coef.T, coef).astype(jnp.bfloat16)
    right = jnp.where(is_text, image16, text16)
    grad_emb = scale * jnp.dot(left, right, preferred_element_type=jnp.float32)
    own = jnp.where(is_text, text, image)
    unit = own[:, :width]
    norm = own[:, width : width + 1] + own[:, width + 1 : width + 2]
    rows = own[:, width + 4 : width + 5]
    grad_pooled = grad_emb - unit * jnp.sum(unit * grad_emb, axis=-1, keepdims=True)
    grad_row = grad_pooled / (norm * rows)
    rows_ref[...] = grad_row
    own_row[...] = rows_ref[pl.ds(pl.multiple_of(flags[2] * 8, 8), 8), :]
    second = w_second[flags[0]]
    columns = contract_last(grad_row.astype(jnp.bfloat16), second)
    for block in range(grad_cols.shape[0]):
        grad_cols[block] = columns[block * 8 : (block + 1) * 8]


def small_call(kernel, outs, operands, scalars, scratch=(), flops=0, moved=0, outside=0):
    single = not isinstance(outs, tuple)
    whole = pl.BlockSpec(memory_space=pltpu.VMEM)
    scalar = pl.BlockSpec(memory_space=pltpu.SMEM)
    return pl.pallas_call(
        kernel,
        in_specs=[scalar] * scalars
        + [whole] * (len(operands) - scalars - outside)
        + [pl.BlockSpec(memory_space=pl.ANY)] * outside,
        out_specs=whole if single else tuple(whole for _ in outs),
        out_shape=outs,
        scratch_shapes=scratch,
        compiler_params=pltpu.CompilerParams(vmem_limit_bytes=16 * 1024 * 1024),
        cost_estimate=pl.CostEstimate(flops=flops, bytes_accessed=moved, transcendentals=0),
    )(*operands)


def ring_body(
    layer_input, caption_ids, positives, ln_gain, w_first, w_second, logit_scale, logit_bias
):
    groups = lax.axis_size("tower")
    tower_index = lax.axis_index("tower")
    block_index = lax.axis_index("blk")
    is_text = tower_index == groups - 1
    row_count, width = layer_input.shape
    slots = caption_ids.shape[0]
    img_count = positives.shape[0] // (groups - 1)
    shard = w_first.shape[2]
    gain = jnp.where(is_text, ln_gain[1], ln_gain[0])
    own = [
        jnp.where(is_text, w_first[1, :, cut].T, w_first[0, :, cut].T)
        for cut in (slice(0, SMALL), slice(SMALL, shard))
    ]
    flags = jnp.stack([is_text.astype(jnp.int32), tower_index * img_count, block_index])
    flags = flags.astype(jnp.int32)
    place = jnp.where(block_index % 2 == 0, block_index // 2, 7 - block_index // 2)
    around = (place + jnp.arange(8, dtype=jnp.int32)) % 8
    block_of = jnp.where(around < 4, 2 * around, 2 * (7 - around) + 1).astype(jnp.int32)

    mask = (caption_ids != 0).astype(jnp.float32)
    counts = jnp.sum(mask, axis=1, keepdims=True)
    row = jnp.arange(row_count, dtype=jnp.int32)[None, :]
    slot = jnp.arange(slots, dtype=jnp.int32)[:, None]
    row_mask = jnp.where(is_text, mask.reshape(1, row_count), 1.0)
    slot_of = jnp.where(is_text, row // TEXT_LEN, tower_index * img_count + row // PATCHES)
    member16 = jnp.where(slot_of == slot, row_mask, 0.0).astype(jnp.bfloat16)
    share = jnp.where(is_text, 1.0 / counts, 1.0 / PATCHES)

    values = layer_input.astype(jnp.float32)
    centered = values - jnp.mean(values, axis=-1, keepdims=True)
    variance = jnp.mean(centered * centered, axis=-1, keepdims=True)
    normed = (centered * lax.rsqrt(variance + norm_eps) * gain).astype(jnp.bfloat16)
    row_mask = row_mask.reshape(row_count, 1)
    arrivals = groups_of(ring_gather(own, groups))
    plan = [(parts, rest) for parts, rest, _ in arrivals]
    share = share.astype(jnp.float32)
    cost = {"flops": int(4e9), "moved": int(16e6)}
    held_shape = jax.ShapeDtypeStruct((8, slots, shard), jnp.float32)
    slopes = []
    held = value_pool = last_pool = None
    for k, (parts, rest, (one, two)) in enumerate(arrivals):
        columns = 3 * SMALL if rest else 2 * SMALL
        slope_shape = jax.ShapeDtypeStruct((row_count, columns), jnp.bfloat16)
        shared = [share, member16]
        weights = [normed, one, two]
        if k == 0:
            slope, held, value_pool = small_call(
                functools.partial(own_kernel, parts, rest),
                (slope_shape, held_shape, jax.ShapeDtypeStruct((slots, width), jnp.float32)),
                [block_of, layer_input, *shared, row_mask, *weights],
                1,
                **cost,
            )
            slopes.append(slope)
        elif k < len(arrivals) - 2:
            slope, held = small_call(
                functools.partial(forward_kernel, parts, rest),
                (slope_shape, held_shape),
                [block_of, held, *shared, row_mask, *weights],
                1,
                **cost,
            )
            slopes.append(slope)
        elif k == len(arrivals) - 2:
            edge_shape = jax.ShapeDtypeStruct((slots, SMALL + REST), jnp.float32)
            slope, *edge_pools = small_call(
                functools.partial(edge_kernel, rest),
                (slope_shape, edge_shape, edge_shape),
                [*shared, row_mask, *weights],
                0,
                **cost,
            )
            slopes.append(slope)
        else:
            last_pool = small_call(
                functools.partial(last_pool_kernel, rest),
                jax.ShapeDtypeStruct((slots, shard), jnp.float32),
                [*shared, *weights],
                0,
                **cost,
            )

    devices = 8 * groups
    pair = slots // groups
    mine = lax.all_to_all(held, "blk", 0, 0)

    def along_ring(value, step):
        routes = []
        for place in range(8):
            for t in range(groups):
                source = RING[place] * groups + t
                routes.append((source, RING[(place + step) % 8] * groups + t))
        return lax.ppermute(value, ("blk", "tower"), routes)

    edges = [along_ring(pool, step) for pool, step in zip(edge_pools, (5, 3))]
    late = along_ring(last_pool, 4)
    partial = small_call(
        partial_kernel,
        jax.ShapeDtypeStruct((devices, pair, width), jnp.bfloat16),
        [flags, block_of, share, value_pool, mine, late, *edges, w_second],
        2,
        (
            pltpu.VMEM((8, slots, shard), jnp.float32),
            pltpu.VMEM((8 * slots, width), jnp.float32),
        ),
    )
    back = lax.all_to_all(partial, ("blk", "tower"), 0, 0)
    _, rest, (one, two) = arrivals[-1]
    slopes.append(
        small_call(
            functools.partial(late_slope_kernel, rest),
            jax.ShapeDtypeStruct((row_count, 3 * SMALL), jnp.bfloat16),
            [row_mask, normed, one, two, partial],
            0,
            flops=int(1e9),
            moved=int(4e6),
            outside=1,
        )
    )

    start = jnp.minimum(tower_index, groups - 2) * img_count
    own_positive = lax.dynamic_slice_in_dim(positives, start, img_count, 0)
    own_counts = lax.dynamic_slice_in_dim(counts[:, 0], tower_index * pair, pair, 0)
    none = jnp.zeros((pair,), jnp.int32)
    notes = jnp.stack(
        [
            jnp.zeros((2 * pair,), jnp.float32),
            jnp.zeros((2 * pair,), jnp.float32),
            jnp.concatenate([own_positive // 64, none]).astype(jnp.float32),
            jnp.concatenate([own_positive % 64, none]).astype(jnp.float32),
            jnp.concatenate([jnp.full((pair,), PATCHES, jnp.float32), own_counts]),
        ],
        axis=1,
    )
    notes = jnp.pad(notes, ((0, 0), (0, 128 - notes.shape[1])))
    copies = small_call(
        functools.partial(embed_kernel, groups),
        jax.ShapeDtypeStruct((devices, 2 * pair, width + 128), jnp.bfloat16),
        [notes, back, slopes[-1]],
        0,
        outside=1,
    )
    packed = lax.all_to_all(copies, ("blk", "tower"), 0, 0)
    packed = packed.reshape(devices * 2 * pair, width + 128)
    grad_cols, own_row = small_call(
        functools.partial(loss_kernel, groups),
        (
            jax.ShapeDtypeStruct((8, slots, shard), jnp.float32),
            jax.ShapeDtypeStruct((slots, width), jnp.float32),
        ),
        [flags, jnp.concatenate([logit_scale, logit_bias]), packed, w_second],
        2,
        (pltpu.VMEM((devices * pair, width), jnp.float32),),
    )
    grad_hidden = lax.all_to_all(grad_cols, "blk", 0, 0)
    return backward_call(
        flags,
        block_of,
        grad_hidden,
        own_row,
        row_mask,
        layer_input,
        gain,
        slopes,
        arrivals,
    )


def general_body(layer_input, caption_ids, positives, ln_gain, w_first, w_second, logit_scale, logit_bias):
    groups = lax.axis_size("tower")
    blocks = lax.axis_size("blk")
    tower_index = lax.axis_index("tower")
    block_index = lax.axis_index("blk")
    is_text = tower_index == groups - 1
    row_count, width = layer_input.shape
    slots = caption_ids.shape[0]
    img_count = positives.shape[0] // (groups - 1)
    shard = w_first.shape[2]
    gain = jnp.where(is_text, ln_gain[1], ln_gain[0])
    first = jnp.where(is_text, w_first[1].T, w_first[0].T)
    second = jnp.where(is_text, w_second[1], w_second[0])

    mask = (caption_ids != 0).astype(jnp.float32)
    counts = jnp.sum(mask, axis=1, keepdims=True)
    row = jnp.arange(row_count, dtype=jnp.int32)[None, :]
    slot = jnp.arange(slots, dtype=jnp.int32)[:, None]
    row_mask = jnp.where(is_text, mask.reshape(1, row_count), 1.0)
    member = jnp.where(jnp.where(is_text, row // TEXT_LEN, row // PATCHES) == slot, row_mask, 0.0)
    share = jnp.where(is_text, 1.0 / counts, 1.0 / PATCHES)
    member16 = member.astype(jnp.bfloat16)

    values = layer_input.astype(jnp.float32)
    centered = values - jnp.mean(values, axis=-1, keepdims=True)
    variance = jnp.mean(centered * centered, axis=-1, keepdims=True)
    inv_std = lax.rsqrt(variance + norm_eps)
    standard = centered * inv_std
    normed = (standard * gain).astype(jnp.bfloat16)
    full = lax.all_gather(first, "blk", axis=0, tiled=True)
    value, slope = gelu_pair(contract_last(normed, full))
    hidden_pool = jnp.dot(member16, value.astype(jnp.bfloat16), preferred_element_type=jnp.float32)
    hidden_pool = hidden_pool * share
    value_pool = jnp.dot(member16, layer_input, preferred_element_type=jnp.float32) * share

    sent = hidden_pool.reshape(slots, blocks, shard).transpose(1, 0, 2)
    mine = lax.all_to_all(sent, "blk", 0, 0).reshape(blocks * slots, shard)
    high, low = two_parts(mine)
    partial = jnp.dot(high, second, preferred_element_type=jnp.float32) + jnp.dot(
        low, second, preferred_element_type=jnp.float32
    )
    back = lax.all_to_all(partial.reshape(blocks, slots, width), "blk", 0, 0)
    pooled = value_pool + jnp.sum(back, axis=0)

    norm = jnp.sqrt(jnp.sum(pooled * pooled, axis=-1, keepdims=True) + norm_eps)
    emb = (pooled / norm).astype(jnp.bfloat16)
    norm_high, norm_low = two_parts(norm)
    start = jnp.minimum(tower_index, groups - 2) * img_count
    own_positive = lax.dynamic_slice_in_dim(positives, start, img_count, 0)
    own_positive = jnp.pad(own_positive, (0, slots - img_count))[:, None]
    extra = jnp.concatenate(
        [
            norm_high,
            norm_low,
            (own_positive // 64).astype(jnp.bfloat16),
            (own_positive % 64).astype(jnp.bfloat16),
            jnp.where(is_text, counts, PATCHES).astype(jnp.bfloat16),
        ],
        axis=1,
    )
    extra = jnp.pad(extra, ((0, 0), (0, 128 - extra.shape[1])))
    packed = jnp.concatenate([emb, extra], axis=1)
    packed = lax.all_to_all(
        jnp.broadcast_to(packed[None], (groups * blocks, *packed.shape)), ("tower", "blk"), 0, 0
    ).reshape(groups * blocks * slots, packed.shape[1])
    every = packed[:, :width]
    notes = packed[:, width : width + 5].astype(jnp.float32)
    every_norm = notes[:, :1] + notes[:, 1:2]
    every_positive = (notes[:, 2:3] * 64.0 + notes[:, 3:4]).astype(jnp.int32)

    scale = logit_scale[0]
    bias = logit_bias[0]
    images = (groups - 1) * blocks * slots
    column = blocks * slots
    text_emb = every[images:]
    logits = scale * contract_last(every[:images], text_emb) + bias
    caption_index = jnp.arange(column, dtype=jnp.int32)[None, :]
    onehot = (every_positive[:images] == caption_index).astype(jnp.float32)
    real = (jnp.arange(images, dtype=jnp.int32) % slots < img_count)[:, None]
    coef = jnp.where(real, loss_scale * (jax.nn.sigmoid(logits) - onehot), 0.0).astype(jnp.bfloat16)
    own = lax.dynamic_slice_in_dim(every, tower_index * column, column, 0)
    own_norm = lax.dynamic_slice_in_dim(every_norm, tower_index * column, column, 0)
    own_coef = lax.dynamic_slice_in_dim(coef, jnp.minimum(tower_index, groups - 2) * column, column, 0)
    grad_image = jnp.dot(own_coef, text_emb, preferred_element_type=jnp.float32)
    grad_text = lax.dot_general(
        coef, every[:images], (((0,), (0,)), ((), ())), preferred_element_type=jnp.float32
    )
    grad_emb = scale * jnp.where(is_text, grad_text, grad_image)
    unit = own.astype(jnp.float32)
    grad_pooled = (grad_emb - unit * jnp.sum(unit * grad_emb, axis=-1, keepdims=True)) / own_norm
    own_rows = lax.dynamic_slice_in_dim(notes[:, 4:5], tower_index * column, column, 0)
    grad_row = grad_pooled / own_rows
    grad_cols = contract_last(grad_row.astype(jnp.bfloat16), second)
    grad_hidden = lax.all_to_all(grad_cols.reshape(blocks, slots, shard), "blk", 0, 0)
    own_row = lax.dynamic_slice_in_dim(grad_row, block_index * slots, slots, 0)
    def spread(rows):
        cols = rows.shape[1]
        image = jnp.broadcast_to(
            rows[:img_count, None, :], (img_count, PATCHES, cols)
        ).reshape(row_count, cols)
        text = (rows[:, None, :] * mask[:, :, None]).reshape(row_count, cols)
        return jnp.where(is_text, text, image)

    grad_hidden = grad_hidden.transpose(1, 0, 2).reshape(slots, blocks * shard)
    grad_out = spread(own_row)
    grad_pre = (spread(grad_hidden) * slope).astype(jnp.bfloat16)
    grad_normed = jnp.dot(grad_pre, full, preferred_element_type=jnp.float32)
    grad_std = grad_normed * gain
    first_mean = jnp.mean(grad_std, axis=-1, keepdims=True)
    second_mean = jnp.mean(grad_std * standard, axis=-1, keepdims=True)
    return grad_out + inv_std * (grad_std - first_mean - standard * second_mean)


def body(layer_input, *others):
    w_first = others[3]
    ring = (
        lax.axis_size("blk") == 8
        and lax.axis_size("tower") == 4
        and w_first.shape[2] == 272
        and others[0].shape[0] == 8
        and others[1].shape[0] == 6
    )
    return (ring_body if ring else general_body)(layer_input, *others)


def solution(mesh):
    placed = (
        P(("blk", "tower"), None),
        P("blk", None),
        P("blk"),
        P(),
        P(None, None, "blk"),
        P(None, "blk", None),
        P(),
        P(),
    )
    return jax.shard_map(
        body, mesh=mesh, in_specs=placed, out_specs=P(("blk", "tower"), None), check_vma=False
    )
```

```python
import functools

import jax
import jax.numpy as jnp
from jax import lax
from jax.experimental import pallas as pl
from jax.experimental.pallas import tpu as pltpu
from jax.sharding import PartitionSpec as P

PATCHES = 256
TEXT_LEN = 64

norm_eps = 1e-06
loss_scale = 128.0
gelu_coeff = 0.7978845608028654


def gelu_pair(pre):
    inner = gelu_coeff * (pre + 0.044715 * pre * pre * pre)
    tanh_part = jnp.tanh(inner)
    value = 0.5 * pre * (1.0 + tanh_part)
    slope = 0.5 * (1.0 + tanh_part) + 0.5 * pre * (1.0 - tanh_part * tanh_part) * gelu_coeff * (
        1.0 + 3.0 * 0.044715 * pre * pre
    )
    return (value, slope)


def contract_last(left, right):
    return lax.dot_general(
        left, right, (((1,), (1,)), ((), ())), preferred_element_type=jnp.float32
    )


def two_parts(value):
    high = value.astype(jnp.bfloat16)
    low = (value - high.astype(jnp.float32)).astype(jnp.bfloat16)
    return high, low


def ring_place(block):
    return block // 2 if block % 2 == 0 else 7 - block // 2


RING = sorted(range(8), key=ring_place)


def ring_gather(own, groups):
    def move(value, step):
        found = []
        for place in range(8):
            for t in range(groups):
                source = RING[place] * groups + t
                found.append((source, RING[(place + step) % 8] * groups + t))
        return lax.ppermute(value, ("blk", "tower"), found)

    pieces = [[None, None] for _ in range(8)]
    pieces[0] = own
    for k in range(1, 5):
        for step in (1, -1):
            for chunk in (0, 1):
                if k == 4 and chunk != (0 if step == 1 else 1):
                    continue
                held = pieces[(-step * (k - 1)) % 8][chunk]
                pieces[(-step * k) % 8][chunk] = move(held, step)
    return pieces


SMALL = 128
REST = 16


def groups_of(pieces):
    found = [([(0, 0), (0, 1)], [0])]
    for k in (1, 2, 3):
        found.append(([(8 - k, 0), (k, 0)], []))
        found.append(([(8 - k, 1), (k, 1)], [8 - k, k]))
    found.append(([(4, 0), (4, 1)], [4]))
    return [(parts, rest, [pieces[p][c] for p, c in parts]) for parts, rest in found]


def project(rest, normed, one, two):
    weights = [one[:SMALL], two[:SMALL]]
    if rest:
        weights += [ref[SMALL:] for ref in (one, two) if ref.shape[0] > SMALL]
    pre = contract_last(normed[...], jnp.concatenate(weights, axis=0))
    square = pre * pre
    tanh_part = jnp.tanh(pre * (gelu_coeff + (gelu_coeff * 0.044715) * square))
    return pre, square, tanh_part, 0.5 + 0.5 * tanh_part


def slope_of(pre, square, tanh_part, gate, mask):
    bend = (0.5 * gelu_coeff) + (0.5 * gelu_coeff * 3.0 * 0.044715) * square
    slope = gate + pre * (1.0 - tanh_part * tanh_part) * bend
    return (slope * mask[...]).astype(jnp.bfloat16)


def pool_of(member, pre, gate):
    hidden = (pre * gate).astype(jnp.bfloat16)
    return jnp.dot(member[...], hidden, preferred_element_type=jnp.float32)


def put_pool(held, block_of, parts, rest, pool):
    for k, (p, c) in enumerate(parts):
        held[block_of[p], :, c * SMALL : (c + 1) * SMALL] = pool[:, k * SMALL : (k + 1) * SMALL]
    for k, p in enumerate(rest):
        start = 2 * SMALL + k * REST
        held[block_of[p], :, 2 * SMALL :] = pool[:, start : start + REST]


def own_kernel(
    parts, rest, block_of, layer_input, share, member, mask, normed, one, two, slope_ref, held, value
):
    pre, square, tanh_part, gate = project(rest, normed, one, two)
    slope = slope_of(pre, square, tanh_part, gate, mask)
    slope_ref[:, : slope.shape[1]] = slope
    held[...] = jnp.zeros_like(held)
    put_pool(held, block_of, parts, rest, pool_of(member, pre, gate) * share[...])
    value[...] = jnp.dot(member[...], layer_input[...], preferred_element_type=jnp.float32)


def forward_kernel(
    parts, rest, block_of, before, share, member, mask, normed, one, two, slope_ref, held
):
    pre, square, tanh_part, gate = project(rest, normed, one, two)
    slope = slope_of(pre, square, tanh_part, gate, mask)
    slope_ref[:, : slope.shape[1]] = slope
    held[...] = before[...]
    put_pool(held, block_of, parts, rest, pool_of(member, pre, gate) * share[...])


def last_pool_kernel(rest, share, member, normed, one, two, pool_ref):
    pre, _, _, gate = project(rest, normed, one, two)
    pool_ref[...] = pool_of(member, pre, gate) * share[...]


def late_slope_kernel(rest, mask, normed, one, two, after, slope_ref):
    slope = slope_of(*project(rest, normed, one, two), mask)
    slope_ref[:, : slope.shape[1]] = slope


def backward_kernel(
    plan, flags, block_of, grad_hidden, own_row, gain, mask, layer_input, *refs
):
    count = len(plan)
    slopes = refs[:count]
    weight_refs = refs[count : 3 * count]
    out = refs[3 * count]
    is_text = flags[0] == 1
    step = pl.program_id(0)
    tile = layer_input.shape[0]
    bands = [pl.ds(k * TEXT_LEN, TEXT_LEN) for k in range(tile // TEXT_LEN)]
    slots = [
        jnp.where(
            is_text,
            step * len(bands) + k,
            flags[1] + (step * len(bands) + k) * TEXT_LEN // PATCHES,
        )
        for k in range(len(bands))
    ]
    def pick(lines, slot):
        row = lax.broadcasted_iota(jnp.int32, lines.shape, 0)
        return jnp.sum(jnp.where(row == slot, lines, 0.0), axis=0, keepdims=True)

    def scaled(slope_ref, start, lines):
        found = []
        for band, slot in zip(bands, slots):
            slope = slope_ref[band, start : start + lines.shape[1]].astype(jnp.float32)
            found.append((pick(lines, slot) * slope).astype(jnp.bfloat16))
        return jnp.concatenate(found, axis=0)

    def multiply(left, parts):
        right = jnp.concatenate(parts, axis=0)
        return jnp.dot(left, right, preferred_element_type=jnp.float32)

    def main_part(g):
        parts, _ = plan[g]
        lines = [grad_hidden[block_of[p], :, c * SMALL : (c + 1) * SMALL] for p, c in parts]
        return scaled(slopes[g], 0, jnp.concatenate(lines, axis=1))

    def rest_part(g):
        _, rest = plan[g]
        lines = [grad_hidden[block_of[p], :, 2 * SMALL :] for p in rest]
        return scaled(slopes[g], 2 * SMALL, jnp.concatenate(lines, axis=1))

    left = [main_part(g) for g in range(count)]
    left += [rest_part(g) for g in range(count) if plan[g][1]]
    parts = [ref[:SMALL] for ref in weight_refs]
    parts += [ref[SMALL:] for ref in weight_refs if ref.shape[0] > SMALL]
    total = multiply(jnp.concatenate(left, axis=1), parts)

    values = layer_input[...].astype(jnp.float32)
    centered = values - jnp.mean(values, axis=-1, keepdims=True)
    variance = jnp.mean(centered * centered, axis=-1, keepdims=True)
    inv_std = lax.rsqrt(variance + norm_eps)
    standard = centered * inv_std
    grad_std = total * gain[...]
    first_mean = jnp.mean(grad_std, axis=-1, keepdims=True)
    second_mean = jnp.mean(grad_std * standard, axis=-1, keepdims=True)
    result = inv_std * (grad_std - first_mean - standard * second_mean)
    for k, (band, slot) in enumerate(zip(bands, slots)):
        grad_out = pick(own_row[...], slot) * mask[band, :]
        out[band, :] = grad_out + result[k * TEXT_LEN : (k + 1) * TEXT_LEN]


def backward_call(flags, block_of, grad_hidden, own_row, mask, layer_input, gain, slopes, groups):
    row_count, width = layer_input.shape
    tile = 2 * TEXT_LEN
    whole = pl.BlockSpec(memory_space=pltpu.VMEM)
    scalar = pl.BlockSpec(memory_space=pltpu.SMEM)

    def by_rows(cols):
        return pl.BlockSpec((tile, cols), lambda i: (i, 0))

    plan = [(parts, rest) for parts, rest, _ in groups]
    weights = [w for _, _, pair in groups for w in pair]
    count = len(plan)
    units = sum(w.shape[0] for w in weights)
    return pl.pallas_call(
        functools.partial(backward_kernel, plan),
        grid=(row_count // tile,),
        in_specs=[scalar] * 2
        + [whole] * 3
        + [by_rows(1), by_rows(width)]
        + [by_rows(slope.shape[1]) for slope in slopes]
        + [whole] * (2 * count),
        out_specs=by_rows(width),
        out_shape=jax.ShapeDtypeStruct((row_count, width), jnp.float32),
        compiler_params=pltpu.CompilerParams(vmem_limit_bytes=60 * 1024 * 1024),
        cost_estimate=pl.CostEstimate(
            flops=2 * row_count * width * units, bytes_accessed=12_000_000, transcendentals=0
        ),
    )(
        flags,
        block_of,
        grad_hidden,
        own_row,
        gain.reshape(1, width),
        mask,
        layer_input,
        *slopes,
        *weights,
    )


def partial_kernel(flags, block_of, share, value_pool, mine, late, w_second, out, pools, rows):
    slots, shard = late.shape
    pools[...] = mine[...]
    pools[block_of[4]] = late[...]
    high, low = two_parts(pools[...].reshape(8 * slots, shard))
    second = w_second[flags[0]]
    both = jnp.dot(
        jnp.concatenate([high, low], axis=0), second, preferred_element_type=jnp.float32
    )
    rows[...] = both[: 8 * slots] + both[8 * slots :]
    own = pl.ds(pl.multiple_of(flags[2] * slots, slots), slots)
    rows[own, :] += value_pool[...] * share[...]
    pair = out.shape[1]
    for k in range(out.shape[0]):
        out[k] = rows[k * pair : (k + 1) * pair, :].astype(out.dtype)


def embed_kernel(groups, notes, back, *refs):
    out = refs[-1]

    def total(places):
        found = back[places[0]].astype(jnp.float32)
        for place in places[1:]:
            found = found + back[place].astype(jnp.float32)
        return found

    devices = range(back.shape[0])
    image = total([d for d in devices if d % groups < groups - 1])
    text = total([d for d in devices if d % groups == groups - 1])
    pooled = jnp.concatenate([image, text], axis=0)
    norm = jnp.sqrt(jnp.sum(pooled * pooled, axis=-1, keepdims=True) + norm_eps)
    emb = (pooled / norm).astype(jnp.bfloat16)
    high = norm.astype(jnp.bfloat16).astype(jnp.float32)
    lane = lax.broadcasted_iota(jnp.int32, notes.shape, 1)
    marks = jnp.where(lane == 0, high, jnp.where(lane == 1, norm - high, notes[...]))
    row = jnp.concatenate([emb, marks.astype(jnp.bfloat16)], axis=1)
    out[...] = jnp.broadcast_to(row[None], out.shape)


def loss_kernel(groups, flags, scalars, packed, w_second, grad_cols, own_row, rows_ref):
    is_text = flags[0] == 1
    scale, bias = scalars[0], scalars[1]
    count, total_width = packed.shape
    width = own_row.shape[1]
    half = count // 2
    row = lax.broadcasted_iota(jnp.int32, (half, count), 0)
    column = lax.broadcasted_iota(jnp.int32, (half, count), 1)
    place = 4 * (row // 2) + row % 2
    everything = packed[...]

    def chosen(offset):
        which = (column == place + offset).astype(jnp.bfloat16)
        return jnp.dot(which, everything, preferred_element_type=jnp.float32)

    image, text = chosen(0), chosen(2)
    image16 = image[:, :width].astype(jnp.bfloat16)
    text16 = text[:, :width].astype(jnp.bfloat16)
    logits = scale * contract_last(image16, text16) + bias
    positive = image[:, width + 2 : width + 3] * 64.0 + image[:, width + 3 : width + 4]
    row = lax.broadcasted_iota(jnp.int32, (half, half), 0)
    column = lax.broadcasted_iota(jnp.int32, (half, half), 1)
    onehot = (column.astype(jnp.float32) == positive).astype(jnp.float32)
    sigmoid = 1.0 / (1.0 + jnp.exp(-logits))
    real = row % (2 * groups) < 2 * (groups - 1)
    coef = jnp.where(real, loss_scale * (sigmoid - onehot), 0.0)
    left = jnp.where(is_text, coef.T, coef).astype(jnp.bfloat16)
    right = jnp.where(is_text, image16, text16)
    grad_emb = scale * jnp.dot(left, right, preferred_element_type=jnp.float32)
    own = jnp.where(is_text, text, image)
    unit = own[:, :width]
    norm = own[:, width : width + 1] + own[:, width + 1 : width + 2]
    rows = own[:, width + 4 : width + 5]
    grad_pooled = grad_emb - unit * jnp.sum(unit * grad_emb, axis=-1, keepdims=True)
    grad_row = grad_pooled / (norm * rows)
    rows_ref[...] = grad_row
    own_row[...] = rows_ref[pl.ds(pl.multiple_of(flags[2] * 8, 8), 8), :]
    second = w_second[flags[0]]
    columns = contract_last(grad_row.astype(jnp.bfloat16), second)
    for block in range(grad_cols.shape[0]):
        grad_cols[block] = columns[block * 8 : (block + 1) * 8]


def small_call(kernel, outs, operands, scalars, scratch=(), flops=0, moved=0, outside=0):
    single = not isinstance(outs, tuple)
    whole = pl.BlockSpec(memory_space=pltpu.VMEM)
    scalar = pl.BlockSpec(memory_space=pltpu.SMEM)
    return pl.pallas_call(
        kernel,
        in_specs=[scalar] * scalars
        + [whole] * (len(operands) - scalars - outside)
        + [pl.BlockSpec(memory_space=pl.ANY)] * outside,
        out_specs=whole if single else tuple(whole for _ in outs),
        out_shape=outs,
        scratch_shapes=scratch,
        compiler_params=pltpu.CompilerParams(vmem_limit_bytes=16 * 1024 * 1024),
        cost_estimate=pl.CostEstimate(flops=flops, bytes_accessed=moved, transcendentals=0),
    )(*operands)


def ring_body(
    layer_input, caption_ids, positives, ln_gain, w_first, w_second, logit_scale, logit_bias
):
    groups = lax.axis_size("tower")
    tower_index = lax.axis_index("tower")
    block_index = lax.axis_index("blk")
    is_text = tower_index == groups - 1
    row_count, width = layer_input.shape
    slots = caption_ids.shape[0]
    img_count = positives.shape[0] // (groups - 1)
    shard = w_first.shape[2]
    gain = jnp.where(is_text, ln_gain[1], ln_gain[0])
    own = [
        jnp.where(is_text, w_first[1, :, cut].T, w_first[0, :, cut].T)
        for cut in (slice(0, SMALL), slice(SMALL, shard))
    ]
    flags = jnp.stack([is_text.astype(jnp.int32), tower_index * img_count, block_index])
    flags = flags.astype(jnp.int32)
    place = jnp.where(block_index % 2 == 0, block_index // 2, 7 - block_index // 2)
    around = (place + jnp.arange(8, dtype=jnp.int32)) % 8
    block_of = jnp.where(around < 4, 2 * around, 2 * (7 - around) + 1).astype(jnp.int32)

    mask = (caption_ids != 0).astype(jnp.float32)
    counts = jnp.sum(mask, axis=1, keepdims=True)
    row = jnp.arange(row_count, dtype=jnp.int32)[None, :]
    slot = jnp.arange(slots, dtype=jnp.int32)[:, None]
    row_mask = jnp.where(is_text, mask.reshape(1, row_count), 1.0)
    slot_of = jnp.where(is_text, row // TEXT_LEN, tower_index * img_count + row // PATCHES)
    member16 = jnp.where(slot_of == slot, row_mask, 0.0).astype(jnp.bfloat16)
    share = jnp.where(is_text, 1.0 / counts, 1.0 / PATCHES)

    values = layer_input.astype(jnp.float32)
    centered = values - jnp.mean(values, axis=-1, keepdims=True)
    variance = jnp.mean(centered * centered, axis=-1, keepdims=True)
    normed = (centered * lax.rsqrt(variance + norm_eps) * gain).astype(jnp.bfloat16)
    row_mask = row_mask.reshape(row_count, 1)
    arrivals = groups_of(ring_gather(own, groups))
    plan = [(parts, rest) for parts, rest, _ in arrivals]
    share = share.astype(jnp.float32)
    cost = {"flops": int(4e9), "moved": int(16e6)}
    held_shape = jax.ShapeDtypeStruct((8, slots, shard), jnp.float32)
    slopes = []
    held = value_pool = last_pool = None
    for k, (parts, rest, (one, two)) in enumerate(arrivals):
        columns = 3 * SMALL if rest else 2 * SMALL
        slope_shape = jax.ShapeDtypeStruct((row_count, columns), jnp.bfloat16)
        shared = [share, member16]
        weights = [normed, one, two]
        if k == 0:
            slope, held, value_pool = small_call(
                functools.partial(own_kernel, parts, rest),
                (slope_shape, held_shape, jax.ShapeDtypeStruct((slots, width), jnp.float32)),
                [block_of, layer_input, *shared, row_mask, *weights],
                1,
                **cost,
            )
            slopes.append(slope)
        elif k < len(arrivals) - 1:
            slope, held = small_call(
                functools.partial(forward_kernel, parts, rest),
                (slope_shape, held_shape),
                [block_of, held, *shared, row_mask, *weights],
                1,
                **cost,
            )
            slopes.append(slope)
        else:
            last_pool = small_call(
                functools.partial(last_pool_kernel, rest),
                jax.ShapeDtypeStruct((slots, shard), jnp.float32),
                [*shared, *weights],
                0,
                **cost,
            )

    devices = 8 * groups
    pair = slots // groups
    mine = lax.all_to_all(held, "blk", 0, 0)
    opposite = []
    for place in range(8):
        for t in range(groups):
            source = RING[place] * groups + t
            opposite.append((source, RING[(place + 4) % 8] * groups + t))
    late = lax.ppermute(last_pool, ("blk", "tower"), opposite)
    partial = small_call(
        partial_kernel,
        jax.ShapeDtypeStruct((devices, pair, width), jnp.bfloat16),
        [flags, block_of, share, value_pool, mine, late, w_second],
        2,
        (
            pltpu.VMEM((8, slots, shard), jnp.float32),
            pltpu.VMEM((8 * slots, width), jnp.float32),
        ),
    )
    back = lax.all_to_all(partial, ("blk", "tower"), 0, 0)
    _, rest, (one, two) = arrivals[-1]
    slopes.append(
        small_call(
            functools.partial(late_slope_kernel, rest),
            jax.ShapeDtypeStruct((row_count, 3 * SMALL), jnp.bfloat16),
            [row_mask, normed, one, two, partial],
            0,
            flops=int(1e9),
            moved=int(4e6),
            outside=1,
        )
    )

    start = jnp.minimum(tower_index, groups - 2) * img_count
    own_positive = lax.dynamic_slice_in_dim(positives, start, img_count, 0)
    own_counts = lax.dynamic_slice_in_dim(counts[:, 0], tower_index * pair, pair, 0)
    none = jnp.zeros((pair,), jnp.int32)
    notes = jnp.stack(
        [
            jnp.zeros((2 * pair,), jnp.float32),
            jnp.zeros((2 * pair,), jnp.float32),
            jnp.concatenate([own_positive // 64, none]).astype(jnp.float32),
            jnp.concatenate([own_positive % 64, none]).astype(jnp.float32),
            jnp.concatenate([jnp.full((pair,), PATCHES, jnp.float32), own_counts]),
        ],
        axis=1,
    )
    notes = jnp.pad(notes, ((0, 0), (0, 128 - notes.shape[1])))
    copies = small_call(
        functools.partial(embed_kernel, groups),
        jax.ShapeDtypeStruct((devices, 2 * pair, width + 128), jnp.bfloat16),
        [notes, back, slopes[-1]],
        0,
        outside=1,
    )
    packed = lax.all_to_all(copies, ("blk", "tower"), 0, 0)
    packed = packed.reshape(devices * 2 * pair, width + 128)
    grad_cols, own_row = small_call(
        functools.partial(loss_kernel, groups),
        (
            jax.ShapeDtypeStruct((8, slots, shard), jnp.float32),
            jax.ShapeDtypeStruct((slots, width), jnp.float32),
        ),
        [flags, jnp.concatenate([logit_scale, logit_bias]), packed, w_second],
        2,
        (pltpu.VMEM((devices * pair, width), jnp.float32),),
    )
    grad_hidden = lax.all_to_all(grad_cols, "blk", 0, 0)
    return backward_call(
        flags,
        block_of,
        grad_hidden,
        own_row,
        row_mask,
        layer_input,
        gain,
        slopes,
        arrivals,
    )


def general_body(layer_input, caption_ids, positives, ln_gain, w_first, w_second, logit_scale, logit_bias):
    groups = lax.axis_size("tower")
    blocks = lax.axis_size("blk")
    tower_index = lax.axis_index("tower")
    block_index = lax.axis_index("blk")
    is_text = tower_index == groups - 1
    row_count, width = layer_input.shape
    slots = caption_ids.shape[0]
    img_count = positives.shape[0] // (groups - 1)
    shard = w_first.shape[2]
    gain = jnp.where(is_text, ln_gain[1], ln_gain[0])
    first = jnp.where(is_text, w_first[1].T, w_first[0].T)
    second = jnp.where(is_text, w_second[1], w_second[0])

    mask = (caption_ids != 0).astype(jnp.float32)
    counts = jnp.sum(mask, axis=1, keepdims=True)
    row = jnp.arange(row_count, dtype=jnp.int32)[None, :]
    slot = jnp.arange(slots, dtype=jnp.int32)[:, None]
    row_mask = jnp.where(is_text, mask.reshape(1, row_count), 1.0)
    member = jnp.where(jnp.where(is_text, row // TEXT_LEN, row // PATCHES) == slot, row_mask, 0.0)
    share = jnp.where(is_text, 1.0 / counts, 1.0 / PATCHES)
    member16 = member.astype(jnp.bfloat16)

    values = layer_input.astype(jnp.float32)
    centered = values - jnp.mean(values, axis=-1, keepdims=True)
    variance = jnp.mean(centered * centered, axis=-1, keepdims=True)
    inv_std = lax.rsqrt(variance + norm_eps)
    standard = centered * inv_std
    normed = (standard * gain).astype(jnp.bfloat16)
    full = lax.all_gather(first, "blk", axis=0, tiled=True)
    value, slope = gelu_pair(contract_last(normed, full))
    hidden_pool = jnp.dot(member16, value.astype(jnp.bfloat16), preferred_element_type=jnp.float32)
    hidden_pool = hidden_pool * share
    value_pool = jnp.dot(member16, layer_input, preferred_element_type=jnp.float32) * share

    sent = hidden_pool.reshape(slots, blocks, shard).transpose(1, 0, 2)
    mine = lax.all_to_all(sent, "blk", 0, 0).reshape(blocks * slots, shard)
    high, low = two_parts(mine)
    partial = jnp.dot(high, second, preferred_element_type=jnp.float32) + jnp.dot(
        low, second, preferred_element_type=jnp.float32
    )
    back = lax.all_to_all(partial.reshape(blocks, slots, width), "blk", 0, 0)
    pooled = value_pool + jnp.sum(back, axis=0)

    norm = jnp.sqrt(jnp.sum(pooled * pooled, axis=-1, keepdims=True) + norm_eps)
    emb = (pooled / norm).astype(jnp.bfloat16)
    norm_high, norm_low = two_parts(norm)
    start = jnp.minimum(tower_index, groups - 2) * img_count
    own_positive = lax.dynamic_slice_in_dim(positives, start, img_count, 0)
    own_positive = jnp.pad(own_positive, (0, slots - img_count))[:, None]
    extra = jnp.concatenate(
        [
            norm_high,
            norm_low,
            (own_positive // 64).astype(jnp.bfloat16),
            (own_positive % 64).astype(jnp.bfloat16),
            jnp.where(is_text, counts, PATCHES).astype(jnp.bfloat16),
        ],
        axis=1,
    )
    extra = jnp.pad(extra, ((0, 0), (0, 128 - extra.shape[1])))
    packed = jnp.concatenate([emb, extra], axis=1)
    packed = lax.all_to_all(
        jnp.broadcast_to(packed[None], (groups * blocks, *packed.shape)), ("tower", "blk"), 0, 0
    ).reshape(groups * blocks * slots, packed.shape[1])
    every = packed[:, :width]
    notes = packed[:, width : width + 5].astype(jnp.float32)
    every_norm = notes[:, :1] + notes[:, 1:2]
    every_positive = (notes[:, 2:3] * 64.0 + notes[:, 3:4]).astype(jnp.int32)

    scale = logit_scale[0]
    bias = logit_bias[0]
    images = (groups - 1) * blocks * slots
    column = blocks * slots
    text_emb = every[images:]
    logits = scale * contract_last(every[:images], text_emb) + bias
    caption_index = jnp.arange(column, dtype=jnp.int32)[None, :]
    onehot = (every_positive[:images] == caption_index).astype(jnp.float32)
    real = (jnp.arange(images, dtype=jnp.int32) % slots < img_count)[:, None]
    coef = jnp.where(real, loss_scale * (jax.nn.sigmoid(logits) - onehot), 0.0).astype(jnp.bfloat16)
    own = lax.dynamic_slice_in_dim(every, tower_index * column, column, 0)
    own_norm = lax.dynamic_slice_in_dim(every_norm, tower_index * column, column, 0)
    own_coef = lax.dynamic_slice_in_dim(coef, jnp.minimum(tower_index, groups - 2) * column, column, 0)
    grad_image = jnp.dot(own_coef, text_emb, preferred_element_type=jnp.float32)
    grad_text = lax.dot_general(
        coef, every[:images], (((0,), (0,)), ((), ())), preferred_element_type=jnp.float32
    )
    grad_emb = scale * jnp.where(is_text, grad_text, grad_image)
    unit = own.astype(jnp.float32)
    grad_pooled = (grad_emb - unit * jnp.sum(unit * grad_emb, axis=-1, keepdims=True)) / own_norm
    own_rows = lax.dynamic_slice_in_dim(notes[:, 4:5], tower_index * column, column, 0)
    grad_row = grad_pooled / own_rows
    grad_cols = contract_last(grad_row.astype(jnp.bfloat16), second)
    grad_hidden = lax.all_to_all(grad_cols.reshape(blocks, slots, shard), "blk", 0, 0)
    own_row = lax.dynamic_slice_in_dim(grad_row, block_index * slots, slots, 0)
    def spread(rows):
        cols = rows.shape[1]
        image = jnp.broadcast_to(
            rows[:img_count, None, :], (img_count, PATCHES, cols)
        ).reshape(row_count, cols)
        text = (rows[:, None, :] * mask[:, :, None]).reshape(row_count, cols)
        return jnp.where(is_text, text, image)

    grad_hidden = grad_hidden.transpose(1, 0, 2).reshape(slots, blocks * shard)
    grad_out = spread(own_row)
    grad_pre = (spread(grad_hidden) * slope).astype(jnp.bfloat16)
    grad_normed = jnp.dot(grad_pre, full, preferred_element_type=jnp.float32)
    grad_std = grad_normed * gain
    first_mean = jnp.mean(grad_std, axis=-1, keepdims=True)
    second_mean = jnp.mean(grad_std * standard, axis=-1, keepdims=True)
    return grad_out + inv_std * (grad_std - first_mean - standard * second_mean)


def body(layer_input, *others):
    w_first = others[3]
    ring = (
        lax.axis_size("blk") == 8
        and lax.axis_size("tower") == 4
        and w_first.shape[2] == 272
        and others[0].shape[0] == 8
        and others[1].shape[0] == 6
    )
    return (ring_body if ring else general_body)(layer_input, *others)


def solution(mesh):
    placed = (
        P(("blk", "tower"), None),
        P("blk", None),
        P("blk"),
        P(),
        P(None, None, "blk"),
        P(None, "blk", None),
        P(),
        P(),
    )
    return jax.shard_map(
        body, mesh=mesh, in_specs=placed, out_specs=P(("blk", "tower"), None), check_vma=False
    )
```

```python
import functools

import jax
import jax.numpy as jnp
from jax import lax
from jax.experimental import pallas as pl
from jax.experimental.pallas import tpu as pltpu
from jax.sharding import PartitionSpec as P

PATCHES = 256
TEXT_LEN = 64

norm_eps = 1e-06
loss_scale = 128.0
gelu_coeff = 0.7978845608028654


def gelu_pair(pre):
    inner = gelu_coeff * (pre + 0.044715 * pre * pre * pre)
    tanh_part = jnp.tanh(inner)
    value = 0.5 * pre * (1.0 + tanh_part)
    slope = 0.5 * (1.0 + tanh_part) + 0.5 * pre * (1.0 - tanh_part * tanh_part) * gelu_coeff * (
        1.0 + 3.0 * 0.044715 * pre * pre
    )
    return (value, slope)


def contract_last(left, right):
    return lax.dot_general(
        left, right, (((1,), (1,)), ((), ())), preferred_element_type=jnp.float32
    )


def two_parts(value):
    high = value.astype(jnp.bfloat16)
    low = (value - high.astype(jnp.float32)).astype(jnp.bfloat16)
    return high, low


def ring_place(block):
    return block // 2 if block % 2 == 0 else 7 - block // 2


RING = sorted(range(8), key=ring_place)


def ring_gather(own, groups):
    def move(value, step):
        found = []
        for place in range(8):
            for t in range(groups):
                source = RING[place] * groups + t
                found.append((source, RING[(place + step) % 8] * groups + t))
        return lax.ppermute(value, ("blk", "tower"), found)

    pieces = [[None, None] for _ in range(8)]
    pieces[0] = own
    for k in range(1, 5):
        for step in (1, -1):
            for chunk in (0, 1):
                if k == 4 and chunk != (0 if step == 1 else 1):
                    continue
                held = pieces[(-step * (k - 1)) % 8][chunk]
                pieces[(-step * k) % 8][chunk] = move(held, step)
    return pieces


SMALL = 128
REST = 16


def groups_of(pieces):
    found = [([(0, 0), (0, 1)], [0])]
    for k in (1, 2, 3):
        found.append(([(8 - k, 0), (k, 0)], []))
        found.append(([(8 - k, 1), (k, 1)], [8 - k, k]))
    found.append(([(4, 0), (4, 1)], [4]))
    return [(parts, rest, [pieces[p][c] for p, c in parts]) for parts, rest in found]


def project(rest, normed, one, two):
    weights = [one[:SMALL], two[:SMALL]]
    if rest:
        weights += [ref[SMALL:] for ref in (one, two) if ref.shape[0] > SMALL]
    pre = contract_last(normed[...], jnp.concatenate(weights, axis=0))
    square = pre * pre
    tanh_part = jnp.tanh(pre * (gelu_coeff + (gelu_coeff * 0.044715) * square))
    return pre, square, tanh_part, 0.5 + 0.5 * tanh_part


def slope_of(pre, square, tanh_part, gate, mask):
    bend = (0.5 * gelu_coeff) + (0.5 * gelu_coeff * 3.0 * 0.044715) * square
    slope = gate + pre * (1.0 - tanh_part * tanh_part) * bend
    return (slope * mask[...]).astype(jnp.bfloat16)


def pool_of(member, pre, gate):
    hidden = (pre * gate).astype(jnp.bfloat16)
    return jnp.dot(member[...], hidden, preferred_element_type=jnp.float32)


def put_pool(held, block_of, parts, rest, pool):
    for k, (p, c) in enumerate(parts):
        held[block_of[p], :, c * SMALL : (c + 1) * SMALL] = pool[:, k * SMALL : (k + 1) * SMALL]
    for k, p in enumerate(rest):
        start = 2 * SMALL + k * REST
        held[block_of[p], :, 2 * SMALL :] = pool[:, start : start + REST]


def own_kernel(
    parts, rest, block_of, layer_input, share, member, mask, normed, one, two, slope_ref, held, value
):
    pre, square, tanh_part, gate = project(rest, normed, one, two)
    slope = slope_of(pre, square, tanh_part, gate, mask)
    slope_ref[:, : slope.shape[1]] = slope
    held[...] = jnp.zeros_like(held)
    put_pool(held, block_of, parts, rest, pool_of(member, pre, gate) * share[...])
    value[...] = jnp.dot(member[...], layer_input[...], preferred_element_type=jnp.float32)


def forward_kernel(
    parts, rest, block_of, before, share, member, mask, normed, one, two, slope_ref, held
):
    pre, square, tanh_part, gate = project(rest, normed, one, two)
    slope = slope_of(pre, square, tanh_part, gate, mask)
    slope_ref[:, : slope.shape[1]] = slope
    held[...] = before[...]
    put_pool(held, block_of, parts, rest, pool_of(member, pre, gate) * share[...])


def last_pool_kernel(rest, share, member, normed, one, two, pool_ref):
    pre, _, _, gate = project(rest, normed, one, two)
    pool_ref[...] = pool_of(member, pre, gate) * share[...]


def late_slope_kernel(rest, mask, normed, one, two, after, slope_ref):
    slope = slope_of(*project(rest, normed, one, two), mask)
    slope_ref[:, : slope.shape[1]] = slope


def backward_kernel(
    plan, flags, block_of, grad_hidden, own_row, gain, mask, layer_input, *refs
):
    count = len(plan)
    slopes = refs[:count]
    weight_refs = refs[count : 3 * count]
    out = refs[3 * count]
    is_text = flags[0] == 1
    step = pl.program_id(0)
    tile = layer_input.shape[0]
    bands = [pl.ds(k * TEXT_LEN, TEXT_LEN) for k in range(tile // TEXT_LEN)]
    slots = [
        jnp.where(
            is_text,
            step * len(bands) + k,
            flags[1] + (step * len(bands) + k) * TEXT_LEN // PATCHES,
        )
        for k in range(len(bands))
    ]
    def pick(lines, slot):
        row = lax.broadcasted_iota(jnp.int32, lines.shape, 0)
        return jnp.sum(jnp.where(row == slot, lines, 0.0), axis=0, keepdims=True)

    def scaled(slope_ref, start, lines):
        found = []
        for band, slot in zip(bands, slots):
            slope = slope_ref[band, start : start + lines.shape[1]].astype(jnp.float32)
            found.append((pick(lines, slot) * slope).astype(jnp.bfloat16))
        return jnp.concatenate(found, axis=0)

    def multiply(left, parts):
        right = jnp.concatenate(parts, axis=0)
        return jnp.dot(left, right, preferred_element_type=jnp.float32)

    def main_part(g):
        parts, _ = plan[g]
        lines = [grad_hidden[block_of[p], :, c * SMALL : (c + 1) * SMALL] for p, c in parts]
        return scaled(slopes[g], 0, jnp.concatenate(lines, axis=1))

    def rest_part(g):
        _, rest = plan[g]
        lines = [grad_hidden[block_of[p], :, 2 * SMALL :] for p in rest]
        return scaled(slopes[g], 2 * SMALL, jnp.concatenate(lines, axis=1))

    rests = [rest_part(g) for g in range(count) if plan[g][1]]
    total = None
    for g in range(0, count, 2):
        left = jnp.concatenate([main_part(g), main_part(g + 1)], axis=1)
        product = multiply(left, [ref[:SMALL] for ref in weight_refs[2 * g : 2 * g + 4]])
        total = product if total is None else total + product
    tails = [ref[SMALL:] for ref in weight_refs if ref.shape[0] > SMALL]
    total = total + multiply(jnp.concatenate(rests, axis=1), tails)

    values = layer_input[...].astype(jnp.float32)
    centered = values - jnp.mean(values, axis=-1, keepdims=True)
    variance = jnp.mean(centered * centered, axis=-1, keepdims=True)
    inv_std = lax.rsqrt(variance + norm_eps)
    standard = centered * inv_std
    grad_std = total * gain[...]
    first_mean = jnp.mean(grad_std, axis=-1, keepdims=True)
    second_mean = jnp.mean(grad_std * standard, axis=-1, keepdims=True)
    result = inv_std * (grad_std - first_mean - standard * second_mean)
    for k, (band, slot) in enumerate(zip(bands, slots)):
        grad_out = pick(own_row[...], slot) * mask[band, :]
        out[band, :] = grad_out + result[k * TEXT_LEN : (k + 1) * TEXT_LEN]


def backward_call(flags, block_of, grad_hidden, own_row, mask, layer_input, gain, slopes, groups):
    row_count, width = layer_input.shape
    tile = 2 * TEXT_LEN
    whole = pl.BlockSpec(memory_space=pltpu.VMEM)
    scalar = pl.BlockSpec(memory_space=pltpu.SMEM)

    def by_rows(cols):
        return pl.BlockSpec((tile, cols), lambda i: (i, 0))

    plan = [(parts, rest) for parts, rest, _ in groups]
    weights = [w for _, _, pair in groups for w in pair]
    count = len(plan)
    units = sum(w.shape[0] for w in weights)
    return pl.pallas_call(
        functools.partial(backward_kernel, plan),
        grid=(row_count // tile,),
        in_specs=[scalar] * 2
        + [whole] * 3
        + [by_rows(1), by_rows(width)]
        + [by_rows(slope.shape[1]) for slope in slopes]
        + [whole] * (2 * count),
        out_specs=by_rows(width),
        out_shape=jax.ShapeDtypeStruct((row_count, width), jnp.float32),
        compiler_params=pltpu.CompilerParams(vmem_limit_bytes=60 * 1024 * 1024),
        cost_estimate=pl.CostEstimate(
            flops=2 * row_count * width * units, bytes_accessed=12_000_000, transcendentals=0
        ),
    )(
        flags,
        block_of,
        grad_hidden,
        own_row,
        gain.reshape(1, width),
        mask,
        layer_input,
        *slopes,
        *weights,
    )


def partial_kernel(flags, block_of, share, value_pool, mine, late, w_second, out, pools, rows):
    slots, shard = late.shape
    pools[...] = mine[...]
    pools[block_of[4]] = late[...]
    high, low = two_parts(pools[...].reshape(8 * slots, shard))
    second = w_second[flags[0]]
    both = jnp.dot(
        jnp.concatenate([high, low], axis=0), second, preferred_element_type=jnp.float32
    )
    rows[...] = both[: 8 * slots] + both[8 * slots :]
    own = pl.ds(pl.multiple_of(flags[2] * slots, slots), slots)
    rows[own, :] += value_pool[...] * share[...]
    pair = out.shape[1]
    for k in range(out.shape[0]):
        out[k] = rows[k * pair : (k + 1) * pair, :].astype(out.dtype)


def embed_kernel(groups, notes, back, *refs):
    out = refs[-1]

    def total(places):
        found = back[places[0]].astype(jnp.float32)
        for place in places[1:]:
            found = found + back[place].astype(jnp.float32)
        return found

    devices = range(back.shape[0])
    image = total([d for d in devices if d % groups < groups - 1])
    text = total([d for d in devices if d % groups == groups - 1])
    pooled = jnp.concatenate([image, text], axis=0)
    norm = jnp.sqrt(jnp.sum(pooled * pooled, axis=-1, keepdims=True) + norm_eps)
    emb = (pooled / norm).astype(jnp.bfloat16)
    high = norm.astype(jnp.bfloat16).astype(jnp.float32)
    lane = lax.broadcasted_iota(jnp.int32, notes.shape, 1)
    marks = jnp.where(lane == 0, high, jnp.where(lane == 1, norm - high, notes[...]))
    row = jnp.concatenate([emb, marks.astype(jnp.bfloat16)], axis=1)
    out[...] = jnp.broadcast_to(row[None], out.shape)


def loss_kernel(groups, flags, scalars, packed, w_second, grad_cols, own_row, rows_ref):
    is_text = flags[0] == 1
    scale, bias = scalars[0], scalars[1]
    count, total_width = packed.shape
    width = own_row.shape[1]
    half = count // 2
    row = lax.broadcasted_iota(jnp.int32, (half, count), 0)
    column = lax.broadcasted_iota(jnp.int32, (half, count), 1)
    place = 4 * (row // 2) + row % 2
    everything = packed[...]

    def chosen(offset):
        which = (column == place + offset).astype(jnp.bfloat16)
        return jnp.dot(which, everything, preferred_element_type=jnp.float32)

    image, text = chosen(0), chosen(2)
    image16 = image[:, :width].astype(jnp.bfloat16)
    text16 = text[:, :width].astype(jnp.bfloat16)
    logits = scale * contract_last(image16, text16) + bias
    positive = image[:, width + 2 : width + 3] * 64.0 + image[:, width + 3 : width + 4]
    row = lax.broadcasted_iota(jnp.int32, (half, half), 0)
    column = lax.broadcasted_iota(jnp.int32, (half, half), 1)
    onehot = (column.astype(jnp.float32) == positive).astype(jnp.float32)
    sigmoid = 1.0 / (1.0 + jnp.exp(-logits))
    real = row % (2 * groups) < 2 * (groups - 1)
    coef = jnp.where(real, loss_scale * (sigmoid - onehot), 0.0)
    left = jnp.where(is_text, coef.T, coef).astype(jnp.bfloat16)
    right = jnp.where(is_text, image16, text16)
    grad_emb = scale * jnp.dot(left, right, preferred_element_type=jnp.float32)
    own = jnp.where(is_text, text, image)
    unit = own[:, :width]
    norm = own[:, width : width + 1] + own[:, width + 1 : width + 2]
    rows = own[:, width + 4 : width + 5]
    grad_pooled = grad_emb - unit * jnp.sum(unit * grad_emb, axis=-1, keepdims=True)
    grad_row = grad_pooled / (norm * rows)
    rows_ref[...] = grad_row
    own_row[...] = rows_ref[pl.ds(pl.multiple_of(flags[2] * 8, 8), 8), :]
    second = w_second[flags[0]]
    columns = contract_last(grad_row.astype(jnp.bfloat16), second)
    for block in range(grad_cols.shape[0]):
        grad_cols[block] = columns[block * 8 : (block + 1) * 8]


def small_call(kernel, outs, operands, scalars, scratch=(), flops=0, moved=0, outside=0):
    single = not isinstance(outs, tuple)
    whole = pl.BlockSpec(memory_space=pltpu.VMEM)
    scalar = pl.BlockSpec(memory_space=pltpu.SMEM)
    return pl.pallas_call(
        kernel,
        in_specs=[scalar] * scalars
        + [whole] * (len(operands) - scalars - outside)
        + [pl.BlockSpec(memory_space=pl.ANY)] * outside,
        out_specs=whole if single else tuple(whole for _ in outs),
        out_shape=outs,
        scratch_shapes=scratch,
        compiler_params=pltpu.CompilerParams(vmem_limit_bytes=16 * 1024 * 1024),
        cost_estimate=pl.CostEstimate(flops=flops, bytes_accessed=moved, transcendentals=0),
    )(*operands)


def ring_body(
    layer_input, caption_ids, positives, ln_gain, w_first, w_second, logit_scale, logit_bias
):
    groups = lax.axis_size("tower")
    tower_index = lax.axis_index("tower")
    block_index = lax.axis_index("blk")
    is_text = tower_index == groups - 1
    row_count, width = layer_input.shape
    slots = caption_ids.shape[0]
    img_count = positives.shape[0] // (groups - 1)
    shard = w_first.shape[2]
    gain = jnp.where(is_text, ln_gain[1], ln_gain[0])
    own = [
        lax.dynamic_index_in_dim(w_first[:, :, cut], is_text.astype(jnp.int32), 0, False).T
        for cut in (slice(0, SMALL), slice(SMALL, shard))
    ]
    flags = jnp.stack([is_text.astype(jnp.int32), tower_index * img_count, block_index])
    flags = flags.astype(jnp.int32)
    place = jnp.where(block_index % 2 == 0, block_index // 2, 7 - block_index // 2)
    around = (place + jnp.arange(8, dtype=jnp.int32)) % 8
    block_of = jnp.where(around < 4, 2 * around, 2 * (7 - around) + 1).astype(jnp.int32)

    mask = (caption_ids != 0).astype(jnp.float32)
    counts = jnp.sum(mask, axis=1, keepdims=True)
    row = jnp.arange(row_count, dtype=jnp.int32)[None, :]
    slot = jnp.arange(slots, dtype=jnp.int32)[:, None]
    row_mask = jnp.where(is_text, mask.reshape(1, row_count), 1.0)
    slot_of = jnp.where(is_text, row // TEXT_LEN, tower_index * img_count + row // PATCHES)
    member16 = jnp.where(slot_of == slot, row_mask, 0.0).astype(jnp.bfloat16)
    share = jnp.where(is_text, 1.0 / counts, 1.0 / PATCHES)

    values = layer_input.astype(jnp.float32)
    centered = values - jnp.mean(values, axis=-1, keepdims=True)
    variance = jnp.mean(centered * centered, axis=-1, keepdims=True)
    normed = (centered * lax.rsqrt(variance + norm_eps) * gain).astype(jnp.bfloat16)
    row_mask = row_mask.reshape(row_count, 1)
    arrivals = groups_of(ring_gather(own, groups))
    plan = [(parts, rest) for parts, rest, _ in arrivals]
    share = share.astype(jnp.float32)
    cost = {"flops": int(4e9), "moved": int(16e6)}
    held_shape = jax.ShapeDtypeStruct((8, slots, shard), jnp.float32)
    slopes = []
    held = value_pool = last_pool = None
    for k, (parts, rest, (one, two)) in enumerate(arrivals):
        columns = 3 * SMALL if rest else 2 * SMALL
        slope_shape = jax.ShapeDtypeStruct((row_count, columns), jnp.bfloat16)
        shared = [share, member16]
        weights = [normed, one, two]
        if k == 0:
            slope, held, value_pool = small_call(
                functools.partial(own_kernel, parts, rest),
                (slope_shape, held_shape, jax.ShapeDtypeStruct((slots, width), jnp.float32)),
                [block_of, layer_input, *shared, row_mask, *weights],
                1,
                **cost,
            )
            slopes.append(slope)
        elif k < len(arrivals) - 1:
            slope, held = small_call(
                functools.partial(forward_kernel, parts, rest),
                (slope_shape, held_shape),
                [block_of, held, *shared, row_mask, *weights],
                1,
                **cost,
            )
            slopes.append(slope)
        else:
            last_pool = small_call(
                functools.partial(last_pool_kernel, rest),
                jax.ShapeDtypeStruct((slots, shard), jnp.float32),
                [*shared, *weights],
                0,
                **cost,
            )

    devices = 8 * groups
    pair = slots // groups
    mine = lax.all_to_all(held, "blk", 0, 0)
    opposite = []
    for place in range(8):
        for t in range(groups):
            source = RING[place] * groups + t
            opposite.append((source, RING[(place + 4) % 8] * groups + t))
    late = lax.ppermute(last_pool, ("blk", "tower"), opposite)
    partial = small_call(
        partial_kernel,
        jax.ShapeDtypeStruct((devices, pair, width), jnp.bfloat16),
        [flags, block_of, share, value_pool, mine, late, w_second],
        2,
        (
            pltpu.VMEM((8, slots, shard), jnp.float32),
            pltpu.VMEM((8 * slots, width), jnp.float32),
        ),
    )
    back = lax.all_to_all(partial, ("blk", "tower"), 0, 0)
    _, rest, (one, two) = arrivals[-1]
    slopes.append(
        small_call(
            functools.partial(late_slope_kernel, rest),
            jax.ShapeDtypeStruct((row_count, 3 * SMALL), jnp.bfloat16),
            [row_mask, normed, one, two, partial],
            0,
            flops=int(1e9),
            moved=int(4e6),
            outside=1,
        )
    )

    start = jnp.minimum(tower_index, groups - 2) * img_count
    own_positive = lax.dynamic_slice_in_dim(positives, start, img_count, 0)
    own_counts = lax.dynamic_slice_in_dim(counts[:, 0], tower_index * pair, pair, 0)
    none = jnp.zeros((pair,), jnp.int32)
    notes = jnp.stack(
        [
            jnp.zeros((2 * pair,), jnp.float32),
            jnp.zeros((2 * pair,), jnp.float32),
            jnp.concatenate([own_positive // 64, none]).astype(jnp.float32),
            jnp.concatenate([own_positive % 64, none]).astype(jnp.float32),
            jnp.concatenate([jnp.full((pair,), PATCHES, jnp.float32), own_counts]),
        ],
        axis=1,
    )
    notes = jnp.pad(notes, ((0, 0), (0, 128 - notes.shape[1])))
    copies = small_call(
        functools.partial(embed_kernel, groups),
        jax.ShapeDtypeStruct((devices, 2 * pair, width + 128), jnp.bfloat16),
        [notes, back, slopes[-1]],
        0,
        outside=1,
    )
    packed = lax.all_to_all(copies, ("blk", "tower"), 0, 0)
    packed = packed.reshape(devices * 2 * pair, width + 128)
    grad_cols, own_row = small_call(
        functools.partial(loss_kernel, groups),
        (
            jax.ShapeDtypeStruct((8, slots, shard), jnp.float32),
            jax.ShapeDtypeStruct((slots, width), jnp.float32),
        ),
        [flags, jnp.concatenate([logit_scale, logit_bias]), packed, w_second],
        2,
        (pltpu.VMEM((devices * pair, width), jnp.float32),),
    )
    grad_hidden = lax.all_to_all(grad_cols, "blk", 0, 0)
    return backward_call(
        flags,
        block_of,
        grad_hidden,
        own_row,
        row_mask,
        layer_input,
        gain,
        slopes,
        arrivals,
    )


def general_body(layer_input, caption_ids, positives, ln_gain, w_first, w_second, logit_scale, logit_bias):
    groups = lax.axis_size("tower")
    blocks = lax.axis_size("blk")
    tower_index = lax.axis_index("tower")
    block_index = lax.axis_index("blk")
    is_text = tower_index == groups - 1
    row_count, width = layer_input.shape
    slots = caption_ids.shape[0]
    img_count = positives.shape[0] // (groups - 1)
    shard = w_first.shape[2]
    gain = jnp.where(is_text, ln_gain[1], ln_gain[0])
    first = jnp.where(is_text, w_first[1].T, w_first[0].T)
    second = jnp.where(is_text, w_second[1], w_second[0])

    mask = (caption_ids != 0).astype(jnp.float32)
    counts = jnp.sum(mask, axis=1, keepdims=True)
    row = jnp.arange(row_count, dtype=jnp.int32)[None, :]
    slot = jnp.arange(slots, dtype=jnp.int32)[:, None]
    row_mask = jnp.where(is_text, mask.reshape(1, row_count), 1.0)
    member = jnp.where(jnp.where(is_text, row // TEXT_LEN, row // PATCHES) == slot, row_mask, 0.0)
    share = jnp.where(is_text, 1.0 / counts, 1.0 / PATCHES)
    member16 = member.astype(jnp.bfloat16)

    values = layer_input.astype(jnp.float32)
    centered = values - jnp.mean(values, axis=-1, keepdims=True)
    variance = jnp.mean(centered * centered, axis=-1, keepdims=True)
    inv_std = lax.rsqrt(variance + norm_eps)
    standard = centered * inv_std
    normed = (standard * gain).astype(jnp.bfloat16)
    full = lax.all_gather(first, "blk", axis=0, tiled=True)
    value, slope = gelu_pair(contract_last(normed, full))
    hidden_pool = jnp.dot(member16, value.astype(jnp.bfloat16), preferred_element_type=jnp.float32)
    hidden_pool = hidden_pool * share
    value_pool = jnp.dot(member16, layer_input, preferred_element_type=jnp.float32) * share

    sent = hidden_pool.reshape(slots, blocks, shard).transpose(1, 0, 2)
    mine = lax.all_to_all(sent, "blk", 0, 0).reshape(blocks * slots, shard)
    high, low = two_parts(mine)
    partial = jnp.dot(high, second, preferred_element_type=jnp.float32) + jnp.dot(
        low, second, preferred_element_type=jnp.float32
    )
    back = lax.all_to_all(partial.reshape(blocks, slots, width), "blk", 0, 0)
    pooled = value_pool + jnp.sum(back, axis=0)

    norm = jnp.sqrt(jnp.sum(pooled * pooled, axis=-1, keepdims=True) + norm_eps)
    emb = (pooled / norm).astype(jnp.bfloat16)
    norm_high, norm_low = two_parts(norm)
    start = jnp.minimum(tower_index, groups - 2) * img_count
    own_positive = lax.dynamic_slice_in_dim(positives, start, img_count, 0)
    own_positive = jnp.pad(own_positive, (0, slots - img_count))[:, None]
    extra = jnp.concatenate(
        [
            norm_high,
            norm_low,
            (own_positive // 64).astype(jnp.bfloat16),
            (own_positive % 64).astype(jnp.bfloat16),
            jnp.where(is_text, counts, PATCHES).astype(jnp.bfloat16),
        ],
        axis=1,
    )
    extra = jnp.pad(extra, ((0, 0), (0, 128 - extra.shape[1])))
    packed = jnp.concatenate([emb, extra], axis=1)
    packed = lax.all_to_all(
        jnp.broadcast_to(packed[None], (groups * blocks, *packed.shape)), ("tower", "blk"), 0, 0
    ).reshape(groups * blocks * slots, packed.shape[1])
    every = packed[:, :width]
    notes = packed[:, width : width + 5].astype(jnp.float32)
    every_norm = notes[:, :1] + notes[:, 1:2]
    every_positive = (notes[:, 2:3] * 64.0 + notes[:, 3:4]).astype(jnp.int32)

    scale = logit_scale[0]
    bias = logit_bias[0]
    images = (groups - 1) * blocks * slots
    column = blocks * slots
    text_emb = every[images:]
    logits = scale * contract_last(every[:images], text_emb) + bias
    caption_index = jnp.arange(column, dtype=jnp.int32)[None, :]
    onehot = (every_positive[:images] == caption_index).astype(jnp.float32)
    real = (jnp.arange(images, dtype=jnp.int32) % slots < img_count)[:, None]
    coef = jnp.where(real, loss_scale * (jax.nn.sigmoid(logits) - onehot), 0.0).astype(jnp.bfloat16)
    own = lax.dynamic_slice_in_dim(every, tower_index * column, column, 0)
    own_norm = lax.dynamic_slice_in_dim(every_norm, tower_index * column, column, 0)
    own_coef = lax.dynamic_slice_in_dim(coef, jnp.minimum(tower_index, groups - 2) * column, column, 0)
    grad_image = jnp.dot(own_coef, text_emb, preferred_element_type=jnp.float32)
    grad_text = lax.dot_general(
        coef, every[:images], (((0,), (0,)), ((), ())), preferred_element_type=jnp.float32
    )
    grad_emb = scale * jnp.where(is_text, grad_text, grad_image)
    unit = own.astype(jnp.float32)
    grad_pooled = (grad_emb - unit * jnp.sum(unit * grad_emb, axis=-1, keepdims=True)) / own_norm
    own_rows = lax.dynamic_slice_in_dim(notes[:, 4:5], tower_index * column, column, 0)
    grad_row = grad_pooled / own_rows
    grad_cols = contract_last(grad_row.astype(jnp.bfloat16), second)
    grad_hidden = lax.all_to_all(grad_cols.reshape(blocks, slots, shard), "blk", 0, 0)
    own_row = lax.dynamic_slice_in_dim(grad_row, block_index * slots, slots, 0)
    def spread(rows):
        cols = rows.shape[1]
        image = jnp.broadcast_to(
            rows[:img_count, None, :], (img_count, PATCHES, cols)
        ).reshape(row_count, cols)
        text = (rows[:, None, :] * mask[:, :, None]).reshape(row_count, cols)
        return jnp.where(is_text, text, image)

    grad_hidden = grad_hidden.transpose(1, 0, 2).reshape(slots, blocks * shard)
    grad_out = spread(own_row)
    grad_pre = (spread(grad_hidden) * slope).astype(jnp.bfloat16)
    grad_normed = jnp.dot(grad_pre, full, preferred_element_type=jnp.float32)
    grad_std = grad_normed * gain
    first_mean = jnp.mean(grad_std, axis=-1, keepdims=True)
    second_mean = jnp.mean(grad_std * standard, axis=-1, keepdims=True)
    return grad_out + inv_std * (grad_std - first_mean - standard * second_mean)


def body(layer_input, *others):
    w_first = others[3]
    ring = (
        lax.axis_size("blk") == 8
        and lax.axis_size("tower") == 4
        and w_first.shape[2] == 272
        and others[0].shape[0] == 8
        and others[1].shape[0] == 6
    )
    return (ring_body if ring else general_body)(layer_input, *others)


def solution(mesh):
    placed = (
        P(("blk", "tower"), None),
        P("blk", None),
        P("blk"),
        P(),
        P(None, None, "blk"),
        P(None, "blk", None),
        P(),
        P(),
    )
    return jax.shard_map(
        body, mesh=mesh, in_specs=placed, out_specs=P(("blk", "tower"), None), check_vma=False
    )
```
